128 devices in a mesh: bx: 8 (over z, x_hi), by: 16 (over y, x_lo, core).
Axes of the slice: x: 4 (x_hi: 2, x_lo: 2; x = x_hi * 2 + x_lo), y: 4, z: 4, core: 2. Of those that a mesh axis runs over, the one named last changes fastest.
Arguments:
- latent: bfloat16 [65536, 128], P(('bx', 'by')), may hold values from -6 to 6
- move_to: int32 [65536], P(('bx', 'by')), may hold values from 0 to 8, as said below
- move_slot: int32 [65536], P(('bx', 'by')), may hold values from 0 to 511, as said below
- arrive_from: int32 [65536], P(('bx', 'by')), may hold values from 0 to 8, as said below
- arrive_slot: int32 [65536], P(('bx', 'by')), may hold values from 0 to 511, as said below
- neighbours: int32 [65536, 16], P(('bx', 'by')), may hold values from 0 to 831
- valid_count: int32 [65536], P(('bx', 'by')), may hold values from 1 to 16
- face_send: int32 [8, 16, 4, 64], P('bx', 'by'), may hold values from 0 to 511
- corner_send: int32 [8, 16, 4, 16], P('bx', 'by'), may hold values from 0 to 511
- edge_in: bfloat16 [2, 2, 128, 128], replicated, may hold values from -0.375 to 0.375
- edge_hid: bfloat16 [2, 2, 128, 128], replicated, may hold values from -0.5 to 0.5
- node_in: bfloat16 [2, 2, 128, 128], replicated, may hold values from -0.375 to 0.375
- node_out: bfloat16 [2, 128, 128], replicated, may hold values from -0.5 to 0.5
- biases: float32 [2, 5, 128], replicated, may hold values from -2 to 2
- gains: float32 [2, 2, 128], replicated, may hold values from 0.5 to 1.5
- grad_out: bfloat16 [65536, 128], P(('bx', 'by')), may hold values from -0.59765625 to 0.59765625
Outputs:
- latent_out: bfloat16 [65536, 128], P(('bx', 'by'))
- grad_latent: bfloat16 [65536, 128], P(('bx', 'by'))
- grad_edge_in: float32 [2, 2, 128, 128], replicated
- grad_edge_hid: float32 [2, 2, 128, 128], replicated
- grad_node_in: float32 [2, 2, 128, 128], replicated
- grad_node_out: float32 [2, 128, 128], replicated
- grad_biases: float32 [2, 5, 128], replicated
- grad_gains: float32 [2, 2, 128], replicated
The draws below stay inside these ranges and needn't reach their ends.
Inputs may be any that keep to these rules, and one draw needn't show every extreme that they name: `move_to`: each particle's direction code of migration; codes other than 4 go to one of the eight bins around. `move_slot`: for a moving particle its slot in the list of its device and direction, 0 to 31, distinct within that list and filling it from 0; for a staying particle its row on the same device after migration. `arrive_from`: for each row after migration the direction code by which it came; with move_to and move_slot the lists describe one permutation of all particles. One device hands at most 32 particles to one neighbour, and some device hands exactly 32 in every draw. `arrive_slot`: for an arrived row its slot in the sender's list for that direction; for a staying row its old row on the same device.
All inputs are finite; a program needn't handle non-finite values.
Results may differ from the reference program's by a relative error of at most 0.025.
Values may be sent and summed in bfloat16 or wider, within the bound.
A program may use at most 128 MiB of HBM per device.

```python
import math
import jax
import jax.numpy as jnp
from jax import lax

D = 128
K = 16
LAYERS = 2
P_SIZE = 512
CAP = 32
HF = 64
HC = 16
LOCAL = 832
NODES = 65536
N_BX = 8
N_BY = 16


TRAVEL = (0, 1, 2, 3, 5, 6, 7, 8)


def migration_plan(key):
    grid_x = N_BX
    grid_y = N_BY
    devices = grid_x * grid_y
    keys = jax.random.split(key, 6)
    base = jax.random.randint(keys[0], (grid_x, grid_y, 4), CAP // 4, CAP + 1)
    spot_x = jax.random.randint(keys[1], (), 0, grid_x)
    spot_y = jax.random.randint(keys[2], (), 0, grid_y)
    spot_code = jax.random.randint(keys[3], (), 0, 4)
    base = base.at[spot_x, spot_y, spot_code].set(CAP).astype(jnp.int32)
    columns = []
    for travel_code in range(9):
        if travel_code < 4:
            columns.append(base[:, :, travel_code])
        elif travel_code == 4:
            columns.append(jnp.zeros((grid_x, grid_y), jnp.int32))
        else:
            columns.append(jnp.roll(base[:, :, 8 - travel_code], (-(travel_code // 3 - 1), -(travel_code % 3 - 1)), axis=(0, 1)))
    arrivals = [jnp.roll(columns[code], (code // 3 - 1, code % 3 - 1), axis=(0, 1)) for code in range(9)]
    sent = jnp.stack([columns[code] for code in TRAVEL], -1).reshape(devices, 8)
    got = jnp.stack([arrivals[code] for code in TRAVEL], -1).reshape(devices, 8)
    moving = jnp.sum(sent, axis=-1)
    sizes_send = jnp.concatenate([sent, (P_SIZE - moving)[:, None]], axis=-1)
    sizes_got = jnp.concatenate([got, (P_SIZE - moving)[:, None]], axis=-1)
    order_codes = jnp.array(TRAVEL + (4,), jnp.int32)
    position = jnp.arange(P_SIZE, dtype=jnp.int32)

    def grouping(sizes):
        ends = jnp.cumsum(sizes, axis=-1)
        group = jnp.sum(position[None, :, None] >= ends[:, None, :], axis=-1).astype(jnp.int32)
        starts = ends - sizes
        offset = position[None, :] - jnp.take_along_axis(starts, group, axis=1)
        return (order_codes[group], offset.astype(jnp.int32), group == 8)
    send_code, send_offset, send_stay = grouping(sizes_send)
    got_code, got_offset, got_stay = grouping(sizes_got)
    old_perm = jax.vmap(lambda one_key: jax.random.permutation(one_key, P_SIZE))(jax.random.split(keys[4], devices)).astype(jnp.int32)
    new_perm = jax.vmap(lambda one_key: jax.random.permutation(one_key, P_SIZE))(jax.random.split(keys[5], devices)).astype(jnp.int32)
    device_rows = jnp.arange(devices, dtype=jnp.int32)[:, None]
    blank = jnp.zeros((devices, P_SIZE), jnp.int32)
    move_to = blank.at[device_rows, old_perm].set(send_code)
    move_slot = blank.at[device_rows, old_perm].set(jnp.where(send_stay, new_perm, send_offset))
    arrive_from = blank.at[device_rows, new_perm].set(got_code)
    arrive_slot = blank.at[device_rows, new_perm].set(jnp.where(got_stay, old_perm, got_offset))
    return (move_to.reshape(-1), move_slot.reshape(-1), arrive_from.reshape(-1), arrive_slot.reshape(-1))


def draw_move_to(key, part):
    return migration_plan(key)[0]


def draw_move_slot(key, part):
    return migration_plan(key)[1]


def draw_arrive_from(key, part):
    return migration_plan(key)[2]


def draw_arrive_slot(key, part):
    return migration_plan(key)[3]


def plant(result, rng, smallest, largest):
    place = [jax.random.randint(jax.random.fold_in(rng, axis), (), 0, length) for axis, length in enumerate(result.shape)]
    widest = result.shape.index(max(result.shape))
    next_to = place[:widest] + [(place[widest] + 1) % result.shape[widest]] + place[widest + 1:]
    return result.at[tuple(place)].set(smallest).at[tuple(next_to)].set(largest)


def shard_levels(own_key, shape, cuts, low, high):
    level, own = 1.0, jax.random.fold_in(own_key, 6)
    for dim, parts in cuts:
        steps = jnp.exp(jax.random.uniform(jax.random.fold_in(own, dim), (parts,), jnp.float32, low / len(cuts), high / len(cuts)))
        level = level * jnp.repeat(steps, shape[dim] // parts).reshape([-1 if axis == dim else 1 for axis in range(len(shape))])
    return level


def bell_draw(rng, extent, scale, reach, cuts=(), kind=jnp.bfloat16):
    loudness = shard_levels(rng, extent, cuts, -0.22, 0.18) if cuts else 1.0
    drawn = jax.random.normal(rng, extent, jnp.float32) * scale * loudness
    return jnp.minimum(jnp.maximum(drawn, -reach), reach).astype(kind)


def setup_inputs(seed: int = 0) -> dict:
    key_list = jax.random.split(jax.random.key(seed), 17)
    return {
        "latent": bell_draw(key_list[0], (NODES, D), 1.0, 6.0, ((0, 128),)),
        "move_to": draw_move_to(jax.random.fold_in(key_list[16], 71), 0),
        "move_slot": draw_move_slot(jax.random.fold_in(key_list[16], 71), 0),
        "arrive_from": draw_arrive_from(jax.random.fold_in(key_list[16], 71), 0),
        "arrive_slot": draw_arrive_slot(jax.random.fold_in(key_list[16], 71), 0),
        "neighbours": plant(jax.random.randint(key_list[5], (NODES, K), 0, LOCAL), jax.random.fold_in(key_list[5], 1), 0, LOCAL - 1).astype(jnp.int32),
        "valid_count": plant(jax.random.randint(key_list[6], (NODES,), 1, K + 1), jax.random.fold_in(key_list[6], 1), 1, K).astype(jnp.int32),
        "face_send": plant(jax.random.randint(key_list[7], (N_BX, N_BY, 4, HF), 0, P_SIZE), jax.random.fold_in(key_list[7], 1), 0, P_SIZE - 1).astype(jnp.int32),
        "corner_send": plant(jax.random.randint(key_list[8], (N_BX, N_BY, 4, HC), 0, P_SIZE), jax.random.fold_in(key_list[8], 1), 0, P_SIZE - 1).astype(jnp.int32),
        "edge_in": bell_draw(key_list[9], (LAYERS, 2, D, D), (2 * D) ** -0.5, 0.375),
        "edge_hid": bell_draw(key_list[10], (LAYERS, 2, D, D), D ** -0.5, 0.5),
        "node_in": bell_draw(key_list[11], (LAYERS, 2, D, D), (2 * D) ** -0.5, 0.375),
        "node_out": bell_draw(key_list[12], (LAYERS, D, D), D ** -0.5, 0.5),
        "biases": bell_draw(key_list[13], (LAYERS, 5, D), 0.3, 2.0, (), jnp.float32),
        "gains": jnp.clip(1.0 + 0.1 * jax.random.normal(key_list[14], (LAYERS, 2, D), jnp.float32), 0.5, 1.5),
        "grad_out": bell_draw(key_list[15], (NODES, D), 0.1, 0.59765625, ((0, 128),)),
    }


def layer_norm(values, gain):
    average = lax.optimization_barrier(jnp.mean(values, axis=-1, keepdims=True))
    centred = values - average
    variance = lax.optimization_barrier(jnp.mean(jnp.square(centred), axis=-1, keepdims=True))
    return centred * lax.rsqrt(variance + 1e-05) * gain

def edge_block(receiver_part, nbr_block, count_block, sender_table, w_mid, w_out, bias_in, bias_mid, bias_out, edge_gain):
    width = receiver_part.shape[-1]
    fanout = nbr_block.shape[-1]
    pre_act = receiver_part[:, None, :] + sender_table[nbr_block] + bias_in
    hidden_one = jax.nn.silu(pre_act).astype(jnp.bfloat16).reshape(-1, width)
    hidden_two = jax.nn.silu(jnp.dot(hidden_one, w_mid, preferred_element_type=jnp.float32) + bias_mid).astype(jnp.bfloat16)
    message = layer_norm(jnp.dot(hidden_two, w_out, preferred_element_type=jnp.float32) + bias_out, edge_gain)
    message = message.reshape(receiver_part.shape[0], fanout, width)
    live = jnp.arange(fanout, dtype=jnp.int32)[None, :] < count_block[:, None]
    return lax.optimization_barrier(jnp.sum(jnp.where(live[:, :, None], message, 0.0), axis=1))

def layer_local(neighbour_rows, valid_count, table, edge_in, edge_hid, node_in, node_out, biases, gains):
    row_count = neighbour_rows.shape[0]
    width = table.shape[-1]
    fanout = neighbour_rows.shape[1]
    table_bf = table.astype(jnp.bfloat16)
    own_rows = table_bf[:row_count]
    receiver_term = jnp.dot(own_rows, edge_in[0].astype(jnp.bfloat16), preferred_element_type=jnp.float32)
    sender_table = jnp.dot(table_bf, edge_in[1].astype(jnp.bfloat16), preferred_element_type=jnp.float32)
    block_rows = math.gcd(row_count, 256)
    blocks = row_count // block_rows
    w_mid = edge_hid[0].astype(jnp.bfloat16)
    w_out = edge_hid[1].astype(jnp.bfloat16)
    checked = jax.checkpoint(edge_block)

    def one_block(pieces):
        return checked(pieces[0], pieces[1], pieces[2], sender_table, w_mid, w_out, biases[0], biases[1], biases[2], gains[0])
    summed = lax.map(one_block, (receiver_term.reshape(blocks, block_rows, width), neighbour_rows.reshape(blocks, block_rows, fanout), valid_count.reshape(blocks, block_rows)))
    aggregate = summed.reshape(row_count, width).astype(jnp.bfloat16)
    node_hidden = jax.nn.silu(jnp.dot(own_rows, node_in[0].astype(jnp.bfloat16), preferred_element_type=jnp.float32) + jnp.dot(aggregate, node_in[1].astype(jnp.bfloat16), preferred_element_type=jnp.float32) + biases[3]).astype(jnp.bfloat16)
    update = layer_norm(jnp.dot(node_hidden, node_out.astype(jnp.bfloat16), preferred_element_type=jnp.float32) + biases[4], gains[1])
    return table[:row_count] + update

def picked(grid, lists):
    return jnp.take_along_axis(grid, lists[..., None], axis=2)

def build_tables(state32, face_send, corner_send):
    grid = state32.reshape(N_BX, N_BY, P_SIZE, -1)
    pieces = [grid]
    for face_idx, moves in enumerate(((1, 0), (-1, 0), (0, 1), (0, -1))):
        pieces.append(jnp.roll(picked(grid, face_send[:, :, face_idx]), moves, axis=(0, 1)))
    for corner_idx, moves in enumerate(((1, 1), (1, -1), (-1, 1), (-1, -1))):
        pieces.append(jnp.roll(picked(grid, corner_send[:, :, corner_idx]), moves, axis=(0, 1)))
    return jnp.concatenate(pieces, axis=2).reshape(N_BX * N_BY, LOCAL, -1)

def migrate(latent, move_to, move_slot, arrive_from, arrive_slot):
    devices = N_BX * N_BY
    row_ids = jnp.arange(NODES, dtype=jnp.int32)
    home = row_ids // P_SIZE
    owner = jnp.zeros((devices, 9, CAP), jnp.int32).at[home, move_to, move_slot].set(row_ids, mode='drop')
    step_x = arrive_from // 3 - 1
    step_y = arrive_from % 3 - 1
    anchor = (home // N_BY - step_x) % N_BX * N_BY + (home % N_BY - step_y) % N_BY
    slot_safe = jnp.minimum(arrive_slot, CAP - 1)
    old_rows = jnp.where(arrive_from == 4, home * P_SIZE + arrive_slot, owner[anchor, arrive_from, slot_safe])
    return latent[old_rows.astype(jnp.int32)]

def reference(latent, move_to, move_slot, arrive_from, arrive_slot, neighbours, valid_count, face_send, corner_send, edge_in, edge_hid, node_in, node_out, biases, gains, grad_out):
    devices = N_BX * N_BY
    nbr_dev = neighbours.reshape(devices, P_SIZE, -1)
    count_dev = valid_count.reshape(devices, P_SIZE)

    def forward(values, weights):
        state = migrate(values, move_to, move_slot, arrive_from, arrive_slot)
        for layer_idx in range(LAYERS):
            weight_set = [weight[layer_idx] for weight in weights]
            tables = build_tables(state.astype(jnp.float32), face_send, corner_send)

            def per_device(pieces, weight_set=weight_set):
                return layer_local(pieces[1], pieces[2], pieces[0], *weight_set)
            results = lax.map(per_device, (tables, nbr_dev, count_dev))
            state = results.reshape(NODES, -1).astype(jnp.bfloat16)
        return state
    weights32 = (edge_in.astype(jnp.float32), edge_hid.astype(jnp.float32), node_in.astype(jnp.float32), node_out.astype(jnp.float32), biases, gains)
    final, pullback = jax.vjp(forward, latent, weights32)
    grad_lat, grad_weights = pullback(grad_out)
    return (final, grad_lat, grad_weights[0], grad_weights[1], grad_weights[2], grad_weights[3], grad_weights[4], grad_weights[5])
```

```python
import functools

import jax
import jax.numpy as jnp
from jax import lax
from jax.experimental import pallas as pl
from jax.experimental.pallas import tpu as pltpu
from jax.sharding import PartitionSpec as P

LAYERS = 2
CAP = 32
D = 128
K = 16
PAIRS = K // 2
ROWS = 512
HALF = 416
HALO = 320
CODES = 9
SLOTS = CODES * CAP
POOL = 384
GRAD_ROWS = 1024
BLOCK = 256
F32 = jnp.float32
BF16 = jnp.bfloat16
MESH = pl.DeviceIdType.MESH
TRAVEL = tuple((code // 3 - 1, code % 3 - 1) for code in range(CODES))
HALO_BLOCKS = (
    (1, 0, 0, 64),
    (-1, 0, 64, 64),
    (0, 1, 128, 64),
    (0, -1, 192, 64),
    (1, 1, 256, 16),
    (1, -1, 272, 16),
    (-1, 1, 288, 16),
    (-1, -1, 304, 16),
)


def dot(a, b):
    return jnp.dot(a, b, preferred_element_type=F32)


def dot_nt(a, b):
    return lax.dot_general(a, b, (((1,), (1,)), ((), ())), preferred_element_type=F32)


def dot_tn(a, b):
    return lax.dot_general(a, b, (((0,), (0,)), ((), ())), preferred_element_type=F32)


def column(row):
    return jnp.transpose(jnp.broadcast_to(row, (D, row.shape[1])))


def one_hot_lanes(filled, width):
    lane = lax.broadcasted_iota(jnp.int32, filled.shape, 1).astype(F32)
    pieces = [
        jnp.where(filled == lane + float(start), 1.0, 0.0).astype(BF16) for start in range(0, width, D)
    ]
    return jnp.concatenate(pieces, axis=1)


def one_hot_rows(row, height):
    index = lax.broadcasted_iota(jnp.int32, (height, row.shape[1]), 0).astype(F32)
    return jnp.where(index == row, 1.0, 0.0).astype(BF16)


def twice(values):
    return jnp.concatenate([values, values], axis=1)


def partial_sums(values):
    return jnp.sum(values.reshape(values.shape[0] // 8, 8, values.shape[1]), axis=0)


def layer_norm_parts(values):
    centred = values - jnp.mean(values, axis=1, keepdims=True)
    scale = lax.rsqrt(jnp.mean(centred * centred, axis=1, keepdims=True) + 1e-05)
    return centred * scale, scale


def half_silu(half):
    wave = jnp.tanh(half)
    gate = 1.0 + wave
    value = half * gate
    return value, gate + value * (1.0 - wave)


def kernel(
    nx, ny,
    lat, move_to, move_slot, arrive_from, arrive_slot, nbr, count, face, corner,
    e_in, e_hid, n_in, n_out, bia, gai, gout,
    state_o, glat_o, gein_o, gehid_o, gnin_o, gnout_o, gbia_o, ggai_o,
    outgoing, arrived, halo_out, halo_in, ret_out, ret_in, back_out, back_in,
    pick_send, pick_back, hits, hits_t, upper, count_col,
    state, recv_term, send_tab, w_mid, w_out, w_mid_t, w_out_t, ones,
    h1s, h2s, d1s, d2s, xhs, rss, acc, agg, nhs, d3s, xh2s, rs2s,
    dxc, g_rows, g_recv, agg_raw, dsend, dw_out, dw_mid, db_out, db_mid,
    terms, rs_in, ar_buf, final,
    mig_s, mig_r, halo_s, halo_r, ret_s, ret_r, back_s, back_r,
    rs_s, rs_r, ar_s, ar_r, ag_s, ag_r,
):
    a = lax.axis_index("bx")
    b = lax.axis_index("by")
    chunk = GRAD_ROWS // ny

    def at(move_x, move_y):
        return (lax.rem(a + (move_x + nx), nx), lax.rem(b + (move_y + ny), ny))

    def remote(src, dst, send, recv, target):
        return pltpu.make_async_remote_copy(
            src_ref=src, dst_ref=dst, send_sem=send, recv_sem=recv, device_id=target, device_id_type=MESH
        )

    barrier = pltpu.get_barrier_semaphore()
    partners = [(0, step) for step in range(1, ny)] + [(step, 0) for step in range(1, nx)]
    partners += [(1, 1), (1, -1), (-1, 1), (-1, -1)]
    for move_x, move_y in partners:
        pl.semaphore_signal(barrier, inc=1, device_id=at(move_x, move_y), device_id_type=MESH)

    def as_row(ref):
        return ref[...].astype(F32)

    to_row, slot_row = as_row(move_to), as_row(move_slot)
    from_row, aslot_row = as_row(arrive_from), as_row(arrive_slot)
    out_target = jnp.where(to_row == 4.0, -1.0, to_row * CAP + slot_row)
    outgoing[...] = dot(one_hot_rows(out_target, SLOTS), lat[...]).astype(BF16)
    arrived[CAP * 4 : CAP * 5, :] = jnp.zeros((CAP, D), BF16)
    arrived[SLOTS:, :] = jnp.zeros((POOL - SLOTS, D), BF16)
    back_in[CAP * 4 : CAP * 5, :] = jnp.zeros((CAP, D), BF16)
    back_in[SLOTS:, :] = jnp.zeros((POOL - SLOTS, D), BF16)
    pl.semaphore_wait(barrier, len(partners))

    def swap_slots(source, target, send, recv, sign):
        copies = []
        for code, (move_x, move_y) in enumerate(TRAVEL):
            if code == 4:
                continue
            rows = pl.ds(code * CAP, CAP)
            copies.append(
                remote(
                    source.at[rows], target.at[rows], send.at[code], recv.at[code],
                    at(sign * move_x, sign * move_y),
                )
            )
        for copy in copies:
            copy.start()
        return copies

    def swap_halo(source, target, send, recv, sign):
        copies = []
        for index, (move_x, move_y, first, size) in enumerate(HALO_BLOCKS):
            rows = pl.ds(first, size)
            copies.append(
                remote(
                    source.at[rows], target.at[rows], send.at[index], recv.at[index],
                    at(sign * move_x, sign * move_y),
                )
            )
        for copy in copies:
            copy.start()
        return copies

    def landed(copies):
        for copy in copies:
            copy.wait_recv()

    everything = []
    migration = swap_slots(outgoing, arrived, mig_s, mig_r, 1)
    everything += migration

    stay_pick = one_hot_lanes(column(jnp.where(from_row == 4.0, aslot_row, -1.0)), ROWS)
    come_pick = one_hot_lanes(column(jnp.where(from_row == 4.0, -1.0, from_row * CAP + aslot_row)), POOL)
    staying = dot(stay_pick, lat[...])
    for index in range(4):
        filled = column(face[index : index + 1, :].astype(F32))
        pick_send[index * 64 : index * 64 + 64, :] = one_hot_lanes(filled, ROWS)
    for index in range(4):
        filled = column(corner[index : index + 1, :].astype(F32))
        pick_send[256 + index * 16 : 272 + index * 16, :] = one_hot_lanes(filled, ROWS)
    pick_back[...] = jnp.transpose(pick_send[...].astype(F32)).astype(BF16)
    count_col[...] = column(as_row(count))

    def build_hits(k, carry):
        row = nbr[pl.ds(k, 1), :].astype(F32)
        high = row >= float(HALF)
        inner = jnp.where(high, row - float(HALF), row)
        hits[k] = one_hot_lanes(column(inner), ROWS)
        upper[k] = column(jnp.where(high, 1.0, 0.0))
        hits_t[k] = one_hot_rows(inner, HALF)
        return carry

    lax.fori_loop(0, K, build_hits, 0)

    diag = (lax.broadcasted_iota(jnp.int32, (2 * D, 2 * D), 0) // D) == (
        lax.broadcasted_iota(jnp.int32, (2 * D, 2 * D), 1) // D
    )
    ones[...] = jnp.where(diag, 1.0 / D, 0.0).astype(BF16)

    def doubled(weight):
        both = jnp.concatenate([twice(weight), twice(weight)], axis=0)
        return jnp.where(diag, both, 0.0).astype(BF16)

    for layer in range(LAYERS):
        mid = e_hid[layer, 0].astype(F32) * 0.5
        out = e_hid[layer, 1].astype(F32)
        w_mid[layer] = doubled(mid)
        w_mid_t[layer] = doubled(jnp.transpose(mid))
        w_out[layer] = doubled(out - jnp.mean(out, axis=1, keepdims=True))
        w_out_t[layer] = doubled(jnp.transpose(out) * 0.5)
    send_tab[HALF:, :] = jnp.zeros((ROWS - HALF, 2 * D), BF16)

    def bias(layer, index):
        return bia[index, layer : layer + 1, :]

    def gain(layer, index):
        return gai[layer, index : index + 1, :]

    landed(migration)
    state[0] = (staying + dot(come_pick, arrived[...])).astype(BF16)

    def forward(layer):
        halo_out[layer] = dot(pick_send[...], state[layer]).astype(BF16)
        halo = swap_halo(halo_out.at[layer], halo_in.at[layer], halo_s.at[layer], halo_r.at[layer], 1)
        everything.extend(halo)
        own = state[layer]
        recv_term[...] = (dot(own, e_in[layer, 0]) + bias(layer, 0)) * 0.5
        w_send = (e_in[layer, 1].astype(F32) * 0.5).astype(BF16)
        own_send = dot(own, w_send).astype(BF16)
        send_tab[0:HALF, 0:D] = own_send[0:HALF]
        send_tab[0 : ROWS - HALF, D:] = own_send[HALF:]
        acc[...] = jnp.zeros((ROWS, D), F32)
        bias_mid = twice(bias(layer, 1)) * 0.5
        bias_out = bias(layer, 2)
        bias_out = twice(bias_out - jnp.mean(bias_out, axis=1, keepdims=True))
        landed(halo)
        send_tab[ROWS - HALF : HALF, D:] = dot(halo_in[layer], w_send).astype(BF16)

        def pair(j, carry):
            low_slot = j.astype(F32)
            for first in range(0, ROWS, BLOCK):
                rows = slice(first, first + BLOCK)
                parts = []
                for k in (j, j + PAIRS):
                    both = dot(hits[k, rows], send_tab[...])
                    parts.append(recv_term[rows] + jnp.where(upper[k, rows] > 0.5, both[:, D:], both[:, :D]))
                value, slope = half_silu(jnp.concatenate(parts, axis=1))
                value = value.astype(BF16)
                h1s[layer, j, rows] = value
                d1s[layer, j, rows] = slope.astype(BF16)
                value, slope = half_silu(dot(value, w_mid[layer]) + bias_mid)
                value = value.astype(BF16)
                h2s[layer, j, rows] = value
                d2s[layer, j, rows] = slope.astype(BF16)
                centred = dot(value, w_out[layer]) + bias_out
                variance = dot((centred * centred).astype(BF16), ones[...])
                scale = lax.rsqrt(variance + 1e-05)
                live = count_col[rows]
                mask = jnp.concatenate([live > low_slot, live > low_slot + PAIRS], axis=1)
                scale = jnp.where(mask, scale, 0.0)
                normed = centred * scale
                rss[layer, j, rows] = scale.astype(BF16)
                xhs[layer, j, rows] = normed.astype(BF16)
                acc[rows] += normed[:, :D] + normed[:, D:]
            return carry

        lax.fori_loop(0, PAIRS, pair, 0)
        total = acc[...]
        agg_raw[layer] = total
        total = (total * gain(layer, 0)).astype(BF16)
        agg[layer] = total
        half = (dot(own, n_in[layer, 0]) + dot(total, n_in[layer, 1]) + bias(layer, 3)) * 0.5
        value, slope = half_silu(half)
        value = value.astype(BF16)
        nhs[layer] = value
        d3s[layer] = slope
        normed, scale = layer_norm_parts(dot(value, n_out[layer]) + bias(layer, 4))
        xh2s[layer] = normed
        rs2s[layer] = jnp.broadcast_to(scale, (ROWS, D))
        return (own.astype(F32) + normed * gain(layer, 1)).astype(BF16)

    for layer in range(LAYERS):
        following = forward(layer)
        if layer + 1 < LAYERS:
            state[layer + 1] = following
        else:
            state_o[...] = following

    def put_term(layer, index, values):
        terms[layer, index * D : index * D + D, :] = values.astype(BF16)

    def put_rows(layer, rows):
        terms[layer, 7 * D :, :] = jnp.zeros((D, D), BF16)
        stacked = jnp.concatenate(rows + [jnp.zeros((9, D), F32)], axis=0)
        terms[layer, 7 * D : 7 * D + 16, :] = stacked.astype(BF16)

    def reduce_start(layer):
        copies = []
        for step in range(1, ny):
            peer = lax.rem(b + step, ny)
            rows = pl.ds(pl.multiple_of(peer * chunk, chunk), chunk)
            copies.append(
                remote(
                    terms.at[layer, rows], rs_in.at[layer, step - 1],
                    rs_s.at[layer, step - 1], rs_r.at[layer, step - 1], (a, peer),
                )
            )
        for copy in copies:
            copy.start()
        everything.extend(copies)
        return copies

    def exchange_start(layer, arriving):
        landed(arriving)
        total = terms[layer, pl.ds(pl.multiple_of(b * chunk, chunk), chunk), :].astype(F32)
        for step in range(ny - 1):
            total = total + rs_in[layer, step].astype(F32)
        ar_buf[layer, a] = total.astype(BF16)
        out, come = [], []
        for step in range(1, nx):
            peer = lax.rem(a + step, nx)
            source = lax.rem(a + (nx - step), nx)
            sems = (ar_s.at[layer, step - 1], ar_r.at[layer, step - 1])
            out.append(remote(ar_buf.at[layer, a], ar_buf.at[layer, a], *sems, (peer, b)))
            come.append(remote(ar_buf.at[layer, source], ar_buf.at[layer, source], *sems, (peer, b)))
        for copy in out:
            copy.start()
        everything.extend(out)
        return come

    def spread_start(layer, arriving):
        landed(arriving)
        total = ar_buf[layer, 0].astype(F32)
        for step in range(1, nx):
            total = total + ar_buf[layer, step].astype(F32)
        final[layer, b] = total.astype(BF16)
        out, come = [], []
        for step in range(1, ny):
            peer = lax.rem(b + step, ny)
            source = lax.rem(b + (ny - step), ny)
            sems = (ag_s.at[layer, step - 1], ag_r.at[layer, step - 1])
            out.append(remote(final.at[layer, b], final.at[layer, b], *sems, (a, peer)))
            come.append(remote(final.at[layer, source], final.at[layer, source], *sems, (a, peer)))
        for copy in out:
            copy.start()
        everything.extend(out)
        return come

    def spread_finish(layer, arriving):
        landed(arriving)
        summed = final[layer].reshape(GRAD_ROWS, D).astype(F32)
        for index in range(2):
            gein_o[layer, index] = summed[index * D : index * D + D]
            gehid_o[layer, index] = summed[(index + 2) * D : (index + 3) * D]
            gnin_o[layer, index] = summed[(index + 4) * D : (index + 5) * D]
        gnout_o[layer] = summed[6 * D : 7 * D]
        gbia_o[layer] = summed[7 * D : 7 * D + 5]
        ggai_o[layer] = summed[7 * D + 5 : 7 * D + 7]

    def backward(layer, cotangent, before_edges):
        own = state[layer]
        normed = xh2s[layer]
        lifted = cotangent * gain(layer, 1)
        grad_gain_node = jnp.sum(cotangent * normed, axis=0, keepdims=True)
        inner = jnp.mean(lifted * normed, axis=1, keepdims=True)
        grad = rs2s[layer] * (lifted - jnp.mean(lifted, axis=1, keepdims=True) - normed * inner)
        grad_b4 = jnp.sum(grad, axis=0, keepdims=True)
        grad = grad.astype(BF16)
        put_term(layer, 6, dot_tn(nhs[layer], grad))
        grad = dot_nt(grad, n_out[layer]) * (d3s[layer] * 0.5)
        grad_b3 = jnp.sum(grad, axis=0, keepdims=True)
        grad = grad.astype(BF16)
        put_term(layer, 4, dot_tn(own, grad))
        put_term(layer, 5, dot_tn(agg[layer], grad))
        own_grad = cotangent + dot_nt(grad, n_in[layer, 0])
        grad_agg = dot_nt(grad, n_in[layer, 1])
        grad_gain_edge = jnp.sum(grad_agg * agg_raw[layer], axis=0, keepdims=True)
        lifted = grad_agg * gain(layer, 0)
        dxc[...] = lifted - jnp.mean(lifted, axis=1, keepdims=True)
        g_recv[...] = jnp.zeros((ROWS, D), F32)
        dsend[...] = jnp.zeros((HALF, 2 * D), F32)
        dw_out[...] = jnp.zeros((D, D), F32)
        dw_mid[...] = jnp.zeros((D, D), F32)
        db_out[...] = jnp.zeros((8, 2 * D), F32)
        db_mid[...] = jnp.zeros((8, 2 * D), F32)
        before_edges()

        def pair(j, carry):
            for first in range(0, ROWS, BLOCK):
                rows = slice(first, first + BLOCK)
                lift = twice(dxc[rows])
                unit = xhs[layer, j, rows].astype(F32)
                shared = dot((lift * unit).astype(BF16), ones[...])
                grad = rss[layer, j, rows].astype(F32) * (lift - unit * shared)
                db_out[...] += partial_sums(grad)
                grad = grad.astype(BF16)
                hidden = h2s[layer, j, rows]
                dw_out[...] += dot_tn(hidden[:, :D], grad[:, :D]) + dot_tn(hidden[:, D:], grad[:, D:])
                grad = dot(grad, w_out_t[layer]) * d2s[layer, j, rows].astype(F32)
                db_mid[...] += partial_sums(grad)
                grad = grad.astype(BF16)
                hidden = h1s[layer, j, rows]
                dw_mid[...] += dot_tn(hidden[:, :D], grad[:, :D]) + dot_tn(hidden[:, D:], grad[:, D:])
                grad = dot(grad, w_mid_t[layer]) * d1s[layer, j, rows].astype(F32)
                g_recv[rows] += grad[:, :D] + grad[:, D:]
                for part in range(2):
                    piece = grad[:, part * D : part * D + D]
                    high = upper[j + part * PAIRS, rows] > 0.5
                    split = jnp.concatenate([jnp.where(high, 0.0, piece), jnp.where(high, piece, 0.0)], axis=1)
                    g_rows[part, rows] = split.astype(BF16)
            dsend[...] += dot(hits_t[j], g_rows[0]) + dot(hits_t[j + PAIRS], g_rows[1])
            return carry

        lax.fori_loop(0, PAIRS, pair, 0)
        send_grad = dsend[...].astype(BF16)
        low = send_grad[:, :D]
        high_own = send_grad[: ROWS - HALF, D:]
        high_halo = send_grad[ROWS - HALF :, D:]
        ret_out[layer] = dot_nt(high_halo, e_in[layer, 1]).astype(BF16)
        returning = swap_halo(ret_out.at[layer], ret_in.at[layer], ret_s.at[layer], ret_r.at[layer], -1)
        everything.extend(returning)
        send_own = jnp.concatenate([low, high_own], axis=0)
        term = dot_tn(own, send_own) + dot_tn(halo_in[layer], high_halo)
        put_term(layer, 1, term)
        grad = g_recv[...]
        grad_b0 = jnp.sum(grad, axis=0, keepdims=True)
        grad = grad.astype(BF16)
        put_term(layer, 0, dot_tn(own, grad))
        put_term(layer, 2, dw_mid[...])
        put_term(layer, 3, dw_out[...])
        total_mid = jnp.sum(db_mid[...], axis=0, keepdims=True)
        total_out = jnp.sum(db_out[...], axis=0, keepdims=True)
        put_rows(
            layer,
            [
                grad_b0,
                total_mid[:, :D] + total_mid[:, D:],
                total_out[:, :D] + total_out[:, D:],
                grad_b3,
                grad_b4,
                grad_gain_edge,
                grad_gain_node,
            ],
        )
        reducing = reduce_start(layer)
        own_grad = own_grad + dot_nt(grad, e_in[layer, 0]) + dot_nt(send_own, e_in[layer, 1])
        landed(returning)
        own_grad = own_grad + dot(pick_back[...], ret_in[layer])
        return own_grad.astype(BF16), reducing

    rounded, reducing_top = backward(1, gout[...].astype(F32), lambda: None)
    exchanging = []
    rounded, reducing_low = backward(
        0, rounded.astype(F32), lambda: exchanging.extend(exchange_start(1, reducing_top))
    )
    spreading_top = spread_start(1, exchanging)

    back_target = jnp.where(from_row == 4.0, -1.0, from_row * CAP + aslot_row)
    back_out[...] = dot(one_hot_rows(back_target, SLOTS), rounded).astype(BF16)
    going_back = swap_slots(back_out, back_in, back_s, back_r, -1)
    everything += going_back
    exchange_low = exchange_start(0, reducing_low)
    stay_pick = one_hot_lanes(column(jnp.where(to_row == 4.0, slot_row, -1.0)), ROWS)
    come_pick = one_hot_lanes(column(out_target), POOL)
    staying = dot(stay_pick, rounded)
    landed(going_back)
    glat_o[...] = (staying + dot(come_pick, back_in[...])).astype(BF16)
    spreading_low = spread_start(0, exchange_low)
    spread_finish(1, spreading_top)
    spread_finish(0, spreading_low)
    for copy in everything:
        copy.wait_send()


def shards(
    latent, move_to, move_slot, arrive_from, arrive_slot, neighbours, valid_count, face_send, corner_send,
    edge_in, edge_hid, node_in, node_out, biases, gains, grad_out,
):
    nx, ny = lax.axis_size("bx"), lax.axis_size("by")
    chunk = GRAD_ROWS // ny
    vmem = pl.BlockSpec(memory_space=pltpu.VMEM)
    shape = jax.ShapeDtypeStruct
    saved = pltpu.VMEM((LAYERS, PAIRS, ROWS, 2 * D), BF16)
    node = pltpu.VMEM((LAYERS, ROWS, D), F32)
    node_bf = pltpu.VMEM((LAYERS, ROWS, D), BF16)
    wide = pltpu.VMEM((LAYERS, 2 * D, 2 * D), BF16)
    dma = pltpu.SemaphoreType.DMA
    scratch = dict(
        outgoing=pltpu.VMEM((SLOTS, D), BF16),
        arrived=pltpu.VMEM((POOL, D), BF16),
        halo_out=pltpu.VMEM((LAYERS, HALO, D), BF16),
        halo_in=pltpu.VMEM((LAYERS, HALO, D), BF16),
        ret_out=pltpu.VMEM((LAYERS, HALO, D), BF16),
        ret_in=pltpu.VMEM((LAYERS, HALO, D), BF16),
        back_out=pltpu.VMEM((SLOTS, D), BF16),
        back_in=pltpu.VMEM((POOL, D), BF16),
        pick_send=pltpu.VMEM((HALO, ROWS), BF16),
        pick_back=pltpu.VMEM((ROWS, HALO), BF16),
        hits=pltpu.VMEM((K, ROWS, ROWS), BF16),
        hits_t=pltpu.VMEM((K, HALF, ROWS), BF16),
        upper=pltpu.VMEM((K, ROWS, D), F32),
        count_col=pltpu.VMEM((ROWS, D), F32),
        state=node_bf,
        recv_term=pltpu.VMEM((ROWS, D), F32),
        send_tab=pltpu.VMEM((ROWS, 2 * D), BF16),
        w_mid=wide,
        w_out=wide,
        w_mid_t=wide,
        w_out_t=wide,
        ones=pltpu.VMEM((2 * D, 2 * D), BF16),
        h1s=saved,
        h2s=saved,
        d1s=saved,
        d2s=saved,
        xhs=saved,
        rss=saved,
        acc=pltpu.VMEM((ROWS, D), F32),
        agg=node_bf,
        nhs=node_bf,
        d3s=node,
        xh2s=node,
        rs2s=node,
        dxc=pltpu.VMEM((ROWS, D), F32),
        g_rows=pltpu.VMEM((2, ROWS, 2 * D), BF16),
        g_recv=pltpu.VMEM((ROWS, D), F32),
        agg_raw=node,
        dsend=pltpu.VMEM((HALF, 2 * D), F32),
        dw_out=pltpu.VMEM((D, D), F32),
        dw_mid=pltpu.VMEM((D, D), F32),
        db_out=pltpu.VMEM((8, 2 * D), F32),
        db_mid=pltpu.VMEM((8, 2 * D), F32),
        terms=pltpu.VMEM((LAYERS, GRAD_ROWS, D), BF16),
        rs_in=pltpu.VMEM((LAYERS, ny - 1, chunk, D), BF16),
        ar_buf=pltpu.VMEM((LAYERS, nx, chunk, D), BF16),
        final=pltpu.VMEM((LAYERS, ny, chunk, D), BF16),
        mig_s=dma((CODES,)),
        mig_r=dma((CODES,)),
        halo_s=dma((LAYERS, 8)),
        halo_r=dma((LAYERS, 8)),
        ret_s=dma((LAYERS, 8)),
        ret_r=dma((LAYERS, 8)),
        back_s=dma((CODES,)),
        back_r=dma((CODES,)),
        rs_s=dma((LAYERS, ny - 1)),
        rs_r=dma((LAYERS, ny - 1)),
        ar_s=dma((LAYERS, nx - 1)),
        ar_r=dma((LAYERS, nx - 1)),
        ag_s=dma((LAYERS, ny - 1)),
        ag_r=dma((LAYERS, ny - 1)),
    )

    def row(values):
        return values.reshape(1, ROWS)

    return pl.pallas_call(
        functools.partial(kernel, nx, ny),
        out_shape=(
            shape((ROWS, D), BF16),
            shape((ROWS, D), BF16),
            shape((LAYERS, 2, D, D), F32),
            shape((LAYERS, 2, D, D), F32),
            shape((LAYERS, 2, D, D), F32),
            shape((LAYERS, D, D), F32),
            shape((LAYERS, 5, D), F32),
            shape((LAYERS, 2, D), F32),
        ),
        in_specs=[vmem] * 16,
        out_specs=(vmem,) * 8,
        scratch_shapes=list(scratch.values()),
        compiler_params=pltpu.CompilerParams(
            collective_id=0, has_side_effects=True, vmem_limit_bytes=60 * 1024 * 1024
        ),
        name="evolve",
    )(
        latent, row(move_to), row(move_slot), row(arrive_from), row(arrive_slot),
        neighbours.T, row(valid_count), face_send.reshape(4, -1), corner_send.reshape(4, -1),
        edge_in, edge_hid, node_in, node_out, biases.transpose(1, 0, 2), gains, grad_out,
    )


def solution(mesh):
    both = ("bx", "by")
    rows, wide, grid = P(both), P(both, None), P("bx", "by", None, None)
    return jax.shard_map(
        shards,
        mesh=mesh,
        in_specs=(wide, rows, rows, rows, rows, wide, rows, grid, grid, P(), P(), P(), P(), P(), P(), wide),
        out_specs=(wide, wide, P(), P(), P(), P(), P(), P()),
        check_vma=False,
    )
```

```python
import functools

import jax
import jax.numpy as jnp
from jax import lax
from jax.experimental import pallas as pl
from jax.experimental.pallas import tpu as pltpu
from jax.sharding import PartitionSpec as P

LAYERS = 2
CAP = 32
D = 128
K = 16
PAIRS = K // 2
ROWS = 512
HALF = 416
HALO = 320
CODES = 9
SLOTS = CODES * CAP
POOL = 384
GRAD_ROWS = 1024
BLOCK = 512
FORWARD_PAIRS = 4
BACKWARD_PAIRS = 4
F32 = jnp.float32
BF16 = jnp.bfloat16
MESH = pl.DeviceIdType.MESH
TRAVEL = tuple((code // 3 - 1, code % 3 - 1) for code in range(CODES))
HALO_BLOCKS = (
    (1, 0, 0, 64),
    (-1, 0, 64, 64),
    (0, 1, 128, 64),
    (0, -1, 192, 64),
    (1, 1, 256, 16),
    (1, -1, 272, 16),
    (-1, 1, 288, 16),
    (-1, -1, 304, 16),
)


def dot(a, b):
    return jnp.dot(a, b, preferred_element_type=F32)


def dot_nt(a, b):
    return lax.dot_general(a, b, (((1,), (1,)), ((), ())), preferred_element_type=F32)


def dot_tn(a, b):
    return lax.dot_general(a, b, (((0,), (0,)), ((), ())), preferred_element_type=F32)


def column(row):
    return jnp.transpose(jnp.broadcast_to(row, (D, row.shape[1])))


def one_hot_lanes(filled, width):
    lane = lax.broadcasted_iota(jnp.int32, filled.shape, 1).astype(F32)
    pieces = [
        jnp.where(filled == lane + float(start), 1.0, 0.0).astype(BF16) for start in range(0, width, D)
    ]
    return jnp.concatenate(pieces, axis=1)


def one_hot_rows(row, height):
    index = lax.broadcasted_iota(jnp.int32, (height, row.shape[1]), 0).astype(F32)
    return jnp.where(index == row, 1.0, 0.0).astype(BF16)


def twice(values):
    return jnp.concatenate([values, values], axis=1)


def partial_sums(values):
    return jnp.sum(values.reshape(values.shape[0] // 8, 8, values.shape[1]), axis=0)


def staggered(chain, pairs):
    def body(group, carry):
        waiting = [
            chain(group * pairs + pair, first) for pair in range(pairs) for first in range(0, ROWS, BLOCK)
        ]
        running = []
        while waiting or running:
            if waiting:
                running.append(waiting.pop(0))
            running = [one for one in running if next(one, True) is None]
        return carry

    lax.fori_loop(0, PAIRS // pairs, body, 0)


def layer_norm_parts(values):
    centred = values - jnp.mean(values, axis=1, keepdims=True)
    scale = lax.rsqrt(jnp.mean(centred * centred, axis=1, keepdims=True) + 1e-05)
    return centred * scale, scale


def half_silu(half):
    wave = jnp.tanh(half)
    gate = 1.0 + wave
    value = half * gate
    return value, gate + value * (1.0 - wave)


def kernel(
    nx, ny,
    lat, move_to, move_slot, arrive_from, arrive_slot, nbr, count, face, corner,
    e_in, e_hid, n_in, n_out, bia, gai, gout,
    state_o, glat_o, gein_o, gehid_o, gnin_o, gnout_o, gbia_o, ggai_o,
    outgoing, arrived, halo_out, halo_in, ret_out, ret_in, back_out, back_in,
    pick_send, pick_back, hits, hits_t, upper, count_col,
    state, recv_term, send_tab, w_mid, w_out, w_mid_t, w_out_t, ones,
    h1s, h2s, d1s, d2s, xhs, rss, acc, agg, nhs, d3s, xh2s, rs2s,
    dxc, g_recv, agg_raw, dsend, dw_out, dw_mid, db_out, db_mid,
    terms, rs_in, ar_buf, final,
    mig_s, mig_r, halo_s, halo_r, ret_s, ret_r, back_s, back_r,
    rs_s, rs_r, ar_s, ar_r, ag_s, ag_r,
):
    a = lax.axis_index("bx")
    b = lax.axis_index("by")
    chunk = GRAD_ROWS // ny

    def at(move_x, move_y):
        return (lax.rem(a + (move_x + nx), nx), lax.rem(b + (move_y + ny), ny))

    def remote(src, dst, send, recv, target):
        return pltpu.make_async_remote_copy(
            src_ref=src, dst_ref=dst, send_sem=send, recv_sem=recv, device_id=target, device_id_type=MESH
        )

    barrier = pltpu.get_barrier_semaphore()
    partners = [(0, step) for step in range(1, ny)] + [(step, 0) for step in range(1, nx)]
    partners += [(1, 1), (1, -1), (-1, 1), (-1, -1)]
    for move_x, move_y in partners:
        pl.semaphore_signal(barrier, inc=1, device_id=at(move_x, move_y), device_id_type=MESH)

    def as_row(ref):
        return ref[...].astype(F32)

    to_row, slot_row = as_row(move_to), as_row(move_slot)
    from_row, aslot_row = as_row(arrive_from), as_row(arrive_slot)
    out_target = jnp.where(to_row == 4.0, -1.0, to_row * CAP + slot_row)
    outgoing[...] = dot(one_hot_rows(out_target, SLOTS), lat[...]).astype(BF16)
    arrived[CAP * 4 : CAP * 5, :] = jnp.zeros((CAP, D), BF16)
    arrived[SLOTS:, :] = jnp.zeros((POOL - SLOTS, D), BF16)
    back_in[CAP * 4 : CAP * 5, :] = jnp.zeros((CAP, D), BF16)
    back_in[SLOTS:, :] = jnp.zeros((POOL - SLOTS, D), BF16)
    pl.semaphore_wait(barrier, len(partners))

    def swap_slots(source, target, send, recv, sign):
        copies = []
        for code, (move_x, move_y) in enumerate(TRAVEL):
            if code == 4:
                continue
            rows = pl.ds(code * CAP, CAP)
            copies.append(
                remote(
                    source.at[rows], target.at[rows], send.at[code], recv.at[code],
                    at(sign * move_x, sign * move_y),
                )
            )
        for copy in copies:
            copy.start()
        return copies

    def swap_halo(source, target, send, recv, sign):
        copies = []
        for index, (move_x, move_y, first, size) in enumerate(HALO_BLOCKS):
            rows = pl.ds(first, size)
            copies.append(
                remote(
                    source.at[rows], target.at[rows], send.at[index], recv.at[index],
                    at(sign * move_x, sign * move_y),
                )
            )
        for copy in copies:
            copy.start()
        return copies

    def landed(copies):
        for copy in copies:
            copy.wait_recv()

    everything = []
    migration = swap_slots(outgoing, arrived, mig_s, mig_r, 1)
    everything += migration

    stay_pick = one_hot_lanes(column(jnp.where(from_row == 4.0, aslot_row, -1.0)), ROWS)
    come_pick = one_hot_lanes(column(jnp.where(from_row == 4.0, -1.0, from_row * CAP + aslot_row)), POOL)
    staying = dot(stay_pick, lat[...])
    for index in range(4):
        filled = column(face[index : index + 1, :].astype(F32))
        pick_send[index * 64 : index * 64 + 64, :] = one_hot_lanes(filled, ROWS)
    for index in range(4):
        filled = column(corner[index : index + 1, :].astype(F32))
        pick_send[256 + index * 16 : 272 + index * 16, :] = one_hot_lanes(filled, ROWS)
    pick_back[...] = jnp.transpose(pick_send[...].astype(F32)).astype(BF16)
    count_col[...] = column(as_row(count))

    def build_hits(k, carry):
        row = nbr[pl.ds(k, 1), :].astype(F32)
        high = row >= float(HALF)
        inner = jnp.where(high, row - float(HALF), row)
        hits[k] = one_hot_lanes(column(inner), ROWS)
        upper[k] = column(jnp.where(high, 1.0, 0.0))
        hits_t[k] = one_hot_rows(inner, HALF)
        return carry

    lax.fori_loop(0, K, build_hits, 0)

    diag = (lax.broadcasted_iota(jnp.int32, (2 * D, 2 * D), 0) // D) == (
        lax.broadcasted_iota(jnp.int32, (2 * D, 2 * D), 1) // D
    )
    ones[...] = jnp.where(diag, 1.0 / D, 0.0).astype(BF16)

    def doubled(weight):
        both = jnp.concatenate([twice(weight), twice(weight)], axis=0)
        return jnp.where(diag, both, 0.0).astype(BF16)

    for layer in range(LAYERS):
        mid = e_hid[layer, 0].astype(F32) * 0.5
        out = e_hid[layer, 1].astype(F32)
        w_mid[layer] = doubled(mid)
        w_mid_t[layer] = doubled(jnp.transpose(mid))
        w_out[layer] = doubled(out - jnp.mean(out, axis=1, keepdims=True))
        w_out_t[layer] = doubled(jnp.transpose(out) * 0.5)
    send_tab[HALF:, :] = jnp.zeros((ROWS - HALF, 2 * D), BF16)

    def bias(layer, index):
        return bia[index, layer : layer + 1, :]

    def gain(layer, index):
        return gai[layer, index : index + 1, :]

    landed(migration)
    state[0] = (staying + dot(come_pick, arrived[...])).astype(BF16)

    def forward(layer):
        halo_out[layer] = dot(pick_send[...], state[layer]).astype(BF16)
        halo = swap_halo(halo_out.at[layer], halo_in.at[layer], halo_s.at[layer], halo_r.at[layer], 1)
        everything.extend(halo)
        own = state[layer]
        recv_term[...] = (dot(own, e_in[layer, 0]) + bias(layer, 0)) * 0.5
        w_send = (e_in[layer, 1].astype(F32) * 0.5).astype(BF16)
        own_send = dot(own, w_send).astype(BF16)
        send_tab[0:HALF, 0:D] = own_send[0:HALF]
        send_tab[0 : ROWS - HALF, D:] = own_send[HALF:]
        acc[...] = jnp.zeros((ROWS, D), F32)
        bias_mid = twice(bias(layer, 1)) * 0.5
        bias_out = bias(layer, 2)
        bias_out = twice(bias_out - jnp.mean(bias_out, axis=1, keepdims=True))
        landed(halo)
        send_tab[ROWS - HALF : HALF, D:] = dot(halo_in[layer], w_send).astype(BF16)

        def chain(j, first):
            rows = slice(first, first + BLOCK)
            both = [dot(hits[k, rows], send_tab[...]) for k in (j, j + PAIRS)]
            yield
            parts = [
                recv_term[rows] + jnp.where(upper[k, rows] > 0.5, pick[:, D:], pick[:, :D])
                for k, pick in zip((j, j + PAIRS), both)
            ]
            value, slope = half_silu(jnp.concatenate(parts, axis=1))
            value = value.astype(BF16)
            h1s[layer, j, rows] = value
            d1s[layer, j, rows] = slope.astype(BF16)
            product = dot(value, w_mid[layer])
            yield
            value, slope = half_silu(product + bias_mid)
            value = value.astype(BF16)
            h2s[layer, j, rows] = value
            d2s[layer, j, rows] = slope.astype(BF16)
            product = dot(value, w_out[layer])
            yield
            centred = product + bias_out
            variance = dot((centred * centred).astype(BF16), ones[...])
            yield
            scale = lax.rsqrt(variance + 1e-05)
            live = count_col[rows]
            low_slot = jnp.float32(j) if isinstance(j, int) else j.astype(F32)
            mask = jnp.concatenate([live > low_slot, live > low_slot + PAIRS], axis=1)
            scale = jnp.where(mask, scale, 0.0)
            normed = centred * scale
            rss[layer, j, rows] = scale.astype(BF16)
            xhs[layer, j, rows] = normed.astype(BF16)
            acc[rows] += normed[:, :D] + normed[:, D:]

        staggered(chain, FORWARD_PAIRS)
        total = acc[...]
        agg_raw[layer] = total
        total = (total * gain(layer, 0)).astype(BF16)
        agg[layer] = total
        half = (dot(own, n_in[layer, 0]) + dot(total, n_in[layer, 1]) + bias(layer, 3)) * 0.5
        value, slope = half_silu(half)
        value = value.astype(BF16)
        nhs[layer] = value
        d3s[layer] = slope
        normed, scale = layer_norm_parts(dot(value, n_out[layer]) + bias(layer, 4))
        xh2s[layer] = normed
        rs2s[layer] = jnp.broadcast_to(scale, (ROWS, D))
        return (own.astype(F32) + normed * gain(layer, 1)).astype(BF16)

    for layer in range(LAYERS):
        following = forward(layer)
        if layer + 1 < LAYERS:
            state[layer + 1] = following
        else:
            state_o[...] = following

    def put_term(layer, index, values):
        terms[layer, index * D : index * D + D, :] = values.astype(BF16)

    def put_rows(layer, rows):
        terms[layer, 7 * D :, :] = jnp.zeros((D, D), BF16)
        stacked = jnp.concatenate(rows + [jnp.zeros((9, D), F32)], axis=0)
        terms[layer, 7 * D : 7 * D + 16, :] = stacked.astype(BF16)

    def reduce_start(layer):
        copies = []
        for step in range(1, ny):
            peer = lax.rem(b + step, ny)
            rows = pl.ds(pl.multiple_of(peer * chunk, chunk), chunk)
            copies.append(
                remote(
                    terms.at[layer, rows], rs_in.at[layer, step - 1],
                    rs_s.at[layer, step - 1], rs_r.at[layer, step - 1], (a, peer),
                )
            )
        for copy in copies:
            copy.start()
        everything.extend(copies)
        return copies

    def exchange_start(layer, arriving):
        landed(arriving)
        total = terms[layer, pl.ds(pl.multiple_of(b * chunk, chunk), chunk), :].astype(F32)
        for step in range(ny - 1):
            total = total + rs_in[layer, step].astype(F32)
        ar_buf[layer, a] = total.astype(BF16)
        out, come = [], []
        for step in range(1, nx):
            peer = lax.rem(a + step, nx)
            source = lax.rem(a + (nx - step), nx)
            sems = (ar_s.at[layer, step - 1], ar_r.at[layer, step - 1])
            out.append(remote(ar_buf.at[layer, a], ar_buf.at[layer, a], *sems, (peer, b)))
            come.append(remote(ar_buf.at[layer, source], ar_buf.at[layer, source], *sems, (peer, b)))
        for copy in out:
            copy.start()
        everything.extend(out)
        return come

    def spread_start(layer, arriving):
        landed(arriving)
        total = ar_buf[layer, 0].astype(F32)
        for step in range(1, nx):
            total = total + ar_buf[layer, step].astype(F32)
        final[layer, b] = total.astype(BF16)
        out, come = [], []
        for step in range(1, ny):
            peer = lax.rem(b + step, ny)
            source = lax.rem(b + (ny - step), ny)
            sems = (ag_s.at[layer, step - 1], ag_r.at[layer, step - 1])
            out.append(remote(final.at[layer, b], final.at[layer, b], *sems, (a, peer)))
            come.append(remote(final.at[layer, source], final.at[layer, source], *sems, (a, peer)))
        for copy in out:
            copy.start()
        everything.extend(out)
        return come

    def spread_finish(layer, arriving):
        landed(arriving)
        summed = final[layer].reshape(GRAD_ROWS, D).astype(F32)
        for index in range(2):
            gein_o[layer, index] = summed[index * D : index * D + D]
            gehid_o[layer, index] = summed[(index + 2) * D : (index + 3) * D]
            gnin_o[layer, index] = summed[(index + 4) * D : (index + 5) * D]
        gnout_o[layer] = summed[6 * D : 7 * D]
        gbia_o[layer] = summed[7 * D : 7 * D + 5]
        ggai_o[layer] = summed[7 * D + 5 : 7 * D + 7]

    def backward(layer, cotangent, before_edges):
        own = state[layer]
        normed = xh2s[layer]
        lifted = cotangent * gain(layer, 1)
        grad_gain_node = jnp.sum(cotangent * normed, axis=0, keepdims=True)
        inner = jnp.mean(lifted * normed, axis=1, keepdims=True)
        grad = rs2s[layer] * (lifted - jnp.mean(lifted, axis=1, keepdims=True) - normed * inner)
        grad_b4 = jnp.sum(grad, axis=0, keepdims=True)
        grad = grad.astype(BF16)
        put_term(layer, 6, dot_tn(nhs[layer], grad))
        grad = dot_nt(grad, n_out[layer]) * (d3s[layer] * 0.5)
        grad_b3 = jnp.sum(grad, axis=0, keepdims=True)
        grad = grad.astype(BF16)
        put_term(layer, 4, dot_tn(own, grad))
        put_term(layer, 5, dot_tn(agg[layer], grad))
        own_grad = cotangent + dot_nt(grad, n_in[layer, 0])
        grad_agg = dot_nt(grad, n_in[layer, 1])
        grad_gain_edge = jnp.sum(grad_agg * agg_raw[layer], axis=0, keepdims=True)
        lifted = grad_agg * gain(layer, 0)
        dxc[...] = lifted - jnp.mean(lifted, axis=1, keepdims=True)
        g_recv[...] = jnp.zeros((ROWS, D), F32)
        dsend[...] = jnp.zeros((HALF, 2 * D), F32)
        dw_out[...] = jnp.zeros((D, D), F32)
        dw_mid[...] = jnp.zeros((D, D), F32)
        db_out[...] = jnp.zeros((8, 2 * D), F32)
        db_mid[...] = jnp.zeros((8, 2 * D), F32)
        before_edges()

        def chain(j, first):
            rows = slice(first, first + BLOCK)
            lift = twice(dxc[rows])
            unit = xhs[layer, j, rows].astype(F32)
            shared = dot((lift * unit).astype(BF16), ones[...])
            yield
            grad = rss[layer, j, rows].astype(F32) * (lift - unit * shared)
            db_out[...] += partial_sums(grad)
            grad = grad.astype(BF16)
            product = dot(grad, w_out_t[layer])
            hidden = h2s[layer, j, rows]
            dw_out[...] += dot_tn(hidden[:, :D], grad[:, :D]) + dot_tn(hidden[:, D:], grad[:, D:])
            yield
            grad = product * d2s[layer, j, rows].astype(F32)
            db_mid[...] += partial_sums(grad)
            grad = grad.astype(BF16)
            product = dot(grad, w_mid_t[layer])
            hidden = h1s[layer, j, rows]
            dw_mid[...] += dot_tn(hidden[:, :D], grad[:, :D]) + dot_tn(hidden[:, D:], grad[:, D:])
            yield
            grad = product * d1s[layer, j, rows].astype(F32)
            g_recv[rows] += grad[:, :D] + grad[:, D:]
            scattered = None
            for part in range(2):
                k = j + part * PAIRS
                piece = grad[:, part * D : part * D + D]
                high = upper[k, rows] > 0.5
                split = jnp.concatenate([jnp.where(high, 0.0, piece), jnp.where(high, piece, 0.0)], axis=1)
                added = dot(hits_t[k, :, rows], split.astype(BF16))
                scattered = added if scattered is None else scattered + added
            dsend[...] += scattered

        staggered(chain, BACKWARD_PAIRS)
        send_grad = dsend[...].astype(BF16)
        low = send_grad[:, :D]
        high_own = send_grad[: ROWS - HALF, D:]
        high_halo = send_grad[ROWS - HALF :, D:]
        ret_out[layer] = dot_nt(high_halo, e_in[layer, 1]).astype(BF16)
        returning = swap_halo(ret_out.at[layer], ret_in.at[layer], ret_s.at[layer], ret_r.at[layer], -1)
        everything.extend(returning)
        send_own = jnp.concatenate([low, high_own], axis=0)
        term = dot_tn(own, send_own) + dot_tn(halo_in[layer], high_halo)
        put_term(layer, 1, term)
        grad = g_recv[...]
        grad_b0 = jnp.sum(grad, axis=0, keepdims=True)
        grad = grad.astype(BF16)
        put_term(layer, 0, dot_tn(own, grad))
        put_term(layer, 2, dw_mid[...])
        put_term(layer, 3, dw_out[...])
        total_mid = jnp.sum(db_mid[...], axis=0, keepdims=True)
        total_out = jnp.sum(db_out[...], axis=0, keepdims=True)
        put_rows(
            layer,
            [
                grad_b0,
                total_mid[:, :D] + total_mid[:, D:],
                total_out[:, :D] + total_out[:, D:],
                grad_b3,
                grad_b4,
                grad_gain_edge,
                grad_gain_node,
            ],
        )
        reducing = reduce_start(layer)
        own_grad = own_grad + dot_nt(grad, e_in[layer, 0]) + dot_nt(send_own, e_in[layer, 1])
        landed(returning)
        own_grad = own_grad + dot(pick_back[...], ret_in[layer])
        return own_grad.astype(BF16), reducing

    rounded, reducing_top = backward(1, gout[...].astype(F32), lambda: None)
    exchanging = []
    rounded, reducing_low = backward(
        0, rounded.astype(F32), lambda: exchanging.extend(exchange_start(1, reducing_top))
    )
    spreading_top = spread_start(1, exchanging)

    back_target = jnp.where(from_row == 4.0, -1.0, from_row * CAP + aslot_row)
    back_out[...] = dot(one_hot_rows(back_target, SLOTS), rounded).astype(BF16)
    going_back = swap_slots(back_out, back_in, back_s, back_r, -1)
    everything += going_back
    exchange_low = exchange_start(0, reducing_low)
    stay_pick = one_hot_lanes(column(jnp.where(to_row == 4.0, slot_row, -1.0)), ROWS)
    come_pick = one_hot_lanes(column(out_target), POOL)
    staying = dot(stay_pick, rounded)
    landed(going_back)
    glat_o[...] = (staying + dot(come_pick, back_in[...])).astype(BF16)
    spreading_low = spread_start(0, exchange_low)
    spread_finish(1, spreading_top)
    spread_finish(0, spreading_low)
    for copy in everything:
        copy.wait_send()


def shards(
    latent, move_to, move_slot, arrive_from, arrive_slot, neighbours, valid_count, face_send, corner_send,
    edge_in, edge_hid, node_in, node_out, biases, gains, grad_out,
):
    nx, ny = lax.axis_size("bx"), lax.axis_size("by")
    chunk = GRAD_ROWS // ny
    vmem = pl.BlockSpec(memory_space=pltpu.VMEM)
    shape = jax.ShapeDtypeStruct
    saved = pltpu.VMEM((LAYERS, PAIRS, ROWS, 2 * D), BF16)
    node = pltpu.VMEM((LAYERS, ROWS, D), F32)
    node_bf = pltpu.VMEM((LAYERS, ROWS, D), BF16)
    wide = pltpu.VMEM((LAYERS, 2 * D, 2 * D), BF16)
    dma = pltpu.SemaphoreType.DMA
    scratch = dict(
        outgoing=pltpu.VMEM((SLOTS, D), BF16),
        arrived=pltpu.VMEM((POOL, D), BF16),
        halo_out=pltpu.VMEM((LAYERS, HALO, D), BF16),
        halo_in=pltpu.VMEM((LAYERS, HALO, D), BF16),
        ret_out=pltpu.VMEM((LAYERS, HALO, D), BF16),
        ret_in=pltpu.VMEM((LAYERS, HALO, D), BF16),
        back_out=pltpu.VMEM((SLOTS, D), BF16),
        back_in=pltpu.VMEM((POOL, D), BF16),
        pick_send=pltpu.VMEM((HALO, ROWS), BF16),
        pick_back=pltpu.VMEM((ROWS, HALO), BF16),
        hits=pltpu.VMEM((K, ROWS, ROWS), BF16),
        hits_t=pltpu.VMEM((K, HALF, ROWS), BF16),
        upper=pltpu.VMEM((K, ROWS, D), F32),
        count_col=pltpu.VMEM((ROWS, D), F32),
        state=node_bf,
        recv_term=pltpu.VMEM((ROWS, D), F32),
        send_tab=pltpu.VMEM((ROWS, 2 * D), BF16),
        w_mid=wide,
        w_out=wide,
        w_mid_t=wide,
        w_out_t=wide,
        ones=pltpu.VMEM((2 * D, 2 * D), BF16),
        h1s=saved,
        h2s=saved,
        d1s=saved,
        d2s=saved,
        xhs=saved,
        rss=saved,
        acc=pltpu.VMEM((ROWS, D), F32),
        agg=node_bf,
        nhs=node_bf,
        d3s=node,
        xh2s=node,
        rs2s=node,
        dxc=pltpu.VMEM((ROWS, D), F32),
        g_recv=pltpu.VMEM((ROWS, D), F32),
        agg_raw=node,
        dsend=pltpu.VMEM((HALF, 2 * D), F32),
        dw_out=pltpu.VMEM((D, D), F32),
        dw_mid=pltpu.VMEM((D, D), F32),
        db_out=pltpu.VMEM((8, 2 * D), F32),
        db_mid=pltpu.VMEM((8, 2 * D), F32),
        terms=pltpu.VMEM((LAYERS, GRAD_ROWS, D), BF16),
        rs_in=pltpu.VMEM((LAYERS, ny - 1, chunk, D), BF16),
        ar_buf=pltpu.VMEM((LAYERS, nx, chunk, D), BF16),
        final=pltpu.VMEM((LAYERS, ny, chunk, D), BF16),
        mig_s=dma((CODES,)),
        mig_r=dma((CODES,)),
        halo_s=dma((LAYERS, 8)),
        halo_r=dma((LAYERS, 8)),
        ret_s=dma((LAYERS, 8)),
        ret_r=dma((LAYERS, 8)),
        back_s=dma((CODES,)),
        back_r=dma((CODES,)),
        rs_s=dma((LAYERS, ny - 1)),
        rs_r=dma((LAYERS, ny - 1)),
        ar_s=dma((LAYERS, nx - 1)),
        ar_r=dma((LAYERS, nx - 1)),
        ag_s=dma((LAYERS, ny - 1)),
        ag_r=dma((LAYERS, ny - 1)),
    )

    def row(values):
        return values.reshape(1, ROWS)

    return pl.pallas_call(
        functools.partial(kernel, nx, ny),
        out_shape=(
            shape((ROWS, D), BF16),
            shape((ROWS, D), BF16),
            shape((LAYERS, 2, D, D), F32),
            shape((LAYERS, 2, D, D), F32),
            shape((LAYERS, 2, D, D), F32),
            shape((LAYERS, D, D), F32),
            shape((LAYERS, 5, D), F32),
            shape((LAYERS, 2, D), F32),
        ),
        in_specs=[vmem] * 16,
        out_specs=(vmem,) * 8,
        scratch_shapes=list(scratch.values()),
        compiler_params=pltpu.CompilerParams(
            collective_id=0, has_side_effects=True, vmem_limit_bytes=60 * 1024 * 1024
        ),
        name="evolve",
    )(
        latent, row(move_to), row(move_slot), row(arrive_from), row(arrive_slot),
        neighbours.T, row(valid_count), face_send.reshape(4, -1), corner_send.reshape(4, -1),
        edge_in, edge_hid, node_in, node_out, biases.transpose(1, 0, 2), gains, grad_out,
    )


def solution(mesh):
    both = ("bx", "by")
    rows, wide, grid = P(both), P(both, None), P("bx", "by", None, None)
    return jax.shard_map(
        shards,
        mesh=mesh,
        in_specs=(wide, rows, rows, rows, rows, wide, rows, grid, grid, P(), P(), P(), P(), P(), P(), wide),
        out_specs=(wide, wide, P(), P(), P(), P(), P(), P()),
        check_vma=False,
    )
```

```python
import functools

import jax
import jax.numpy as jnp
from jax import lax
from jax.experimental import pallas as pl
from jax.experimental.pallas import tpu as pltpu
from jax.sharding import PartitionSpec as P

LAYERS = 2
CAP = 32
D = 128
K = 16
PAIRS = K // 2
ROWS = 512
HALF = 416
HALO = 320
CODES = 9
SLOTS = CODES * CAP
POOL = 384
EARLY_ROWS = 1280
LATE_ROWS = 768
LATE_VECTORS = 512
BLOCK = 512
FORWARD_PAIRS = 4
BACKWARD_PAIRS = 4
F32 = jnp.float32
BF16 = jnp.bfloat16
MESH = pl.DeviceIdType.MESH
TRAVEL = tuple((code // 3 - 1, code % 3 - 1) for code in range(CODES))
HALO_BLOCKS = (
    (1, 0, 0, 64),
    (-1, 0, 64, 64),
    (0, 1, 128, 64),
    (0, -1, 192, 64),
    (1, 1, 256, 16),
    (1, -1, 272, 16),
    (-1, 1, 288, 16),
    (-1, -1, 304, 16),
)

ARGUMENTS = (
    "lat", "move_to", "move_slot", "arrive_from", "arrive_slot", "nbr", "count", "face", "corner",
    "e_in", "e_hid", "n_in", "n_out", "bia", "gai", "gout",
)
RESULTS = ("state_o", "glat_o", "early_o", "late_o")
SCRATCH = (
    "outgoing", "arrived", "halo_out", "halo_in", "ret_out", "ret_in", "back_out", "back_in",
    "pick_send", "pick_back", "hits", "hits_t", "upper", "count_col", "state", "recv_term",
    "send_tab", "w_mid", "w_out", "w_mid_t", "w_out_t", "ones", "h1s", "h2s", "d1s", "d2s", "xhs",
    "rss", "acc", "agg", "nhs", "d3s", "xh2s", "rs2s", "dxc", "g_recv", "agg_raw", "dsend",
    "dw_out", "dw_mid", "db_out", "db_mid", "mig_s", "mig_r", "halo_s", "halo_r", "ret_s", "ret_r",
    "back_s", "back_r",
)
EDGE_GROUPS = ("late", "early")
NODE_TERMS = (7, 4)


def dot(a, b):
    return jnp.dot(a, b, preferred_element_type=F32)


def dot_nt(a, b):
    return lax.dot_general(a, b, (((1,), (1,)), ((), ())), preferred_element_type=F32)


def dot_tn(a, b):
    return lax.dot_general(a, b, (((0,), (0,)), ((), ())), preferred_element_type=F32)


def column(row):
    return jnp.transpose(jnp.broadcast_to(row, (D, row.shape[1])))


def one_hot_lanes(filled, width):
    lane = lax.broadcasted_iota(jnp.int32, filled.shape, 1).astype(F32)
    pieces = [
        jnp.where(filled == lane + float(start), 1.0, 0.0).astype(BF16) for start in range(0, width, D)
    ]
    return jnp.concatenate(pieces, axis=1)


def one_hot_rows(row, height):
    index = lax.broadcasted_iota(jnp.int32, (height, row.shape[1]), 0).astype(F32)
    return jnp.where(index == row, 1.0, 0.0).astype(BF16)


def twice(values):
    return jnp.concatenate([values, values], axis=1)


def partial_sums(values):
    return jnp.sum(values.reshape(values.shape[0] // 8, 8, values.shape[1]), axis=0)


def staggered(chain, pairs):
    def body(group, carry):
        waiting = [
            chain(group * pairs + pair, first) for pair in range(pairs) for first in range(0, ROWS, BLOCK)
        ]
        running = []
        while waiting or running:
            if waiting:
                running.append(waiting.pop(0))
            running = [one for one in running if next(one, True) is None]
        return carry

    lax.fori_loop(0, PAIRS // pairs, body, 0)


def layer_norm_parts(values):
    centred = values - jnp.mean(values, axis=1, keepdims=True)
    scale = lax.rsqrt(jnp.mean(centred * centred, axis=1, keepdims=True) + 1e-05)
    return centred * scale, scale


def half_silu(half):
    wave = jnp.tanh(half)
    gate = 1.0 + wave
    value = half * gate
    return value, gate + value * (1.0 - wave)


def kernel(
    nx, ny, names, *refs
):
    refs = dict(zip(names, refs))
    arguments = [(refs["arg_" + name], refs[name]) for name in ARGUMENTS]
    (
        lat, move_to, move_slot, arrive_from, arrive_slot, nbr, count, face, corner,
        e_in, e_hid, n_in, n_out, bia, gai, gout,
    ) = (local for _, local in arguments)
    state_o, glat_o, early_o, late_o = (refs[name] for name in RESULTS)
    (
        outgoing, arrived, halo_out, halo_in, ret_out, ret_in, back_out, back_in,
        pick_send, pick_back, hits, hits_t, upper, count_col,
        state, recv_term, send_tab, w_mid, w_out, w_mid_t, w_out_t, ones,
        h1s, h2s, d1s, d2s, xhs, rss, acc, agg, nhs, d3s, xh2s, rs2s,
        dxc, g_recv, agg_raw, dsend, dw_out, dw_mid, db_out, db_mid,
        mig_s, mig_r, halo_s, halo_r, ret_s, ret_r, back_s, back_r,
    ) = (refs[name] for name in SCRATCH)
    a = lax.axis_index("bx")
    b = lax.axis_index("by")

    def at(move_x, move_y):
        return (lax.rem(a + (move_x + nx), nx), lax.rem(b + (move_y + ny), ny))

    def remote(src, dst, send, recv, target):
        return pltpu.make_async_remote_copy(
            src_ref=src, dst_ref=dst, send_sem=send, recv_sem=recv, device_id=target, device_id_type=MESH
        )

    barrier = pltpu.get_barrier_semaphore()
    partners = [(0, step) for step in range(1, ny)] + [(step, 0) for step in range(1, nx)]
    partners += [(1, 1), (1, -1), (-1, 1), (-1, -1)]
    for move_x, move_y in partners:
        pl.semaphore_signal(barrier, inc=1, device_id=at(move_x, move_y), device_id_type=MESH)

    loads = [
        pltpu.make_async_copy(there, here, refs["load_s"].at[index])
        for index, (there, here) in enumerate(arguments)
    ]
    for load in loads:
        load.start()
    for load in loads[:9]:
        load.wait()

    def as_row(ref):
        return ref[...].astype(F32)

    to_row, slot_row = as_row(move_to), as_row(move_slot)
    from_row, aslot_row = as_row(arrive_from), as_row(arrive_slot)
    out_target = jnp.where(to_row == 4.0, -1.0, to_row * CAP + slot_row)
    outgoing[...] = dot(one_hot_rows(out_target, SLOTS), lat[...]).astype(BF16)
    arrived[CAP * 4 : CAP * 5, :] = jnp.zeros((CAP, D), BF16)
    arrived[SLOTS:, :] = jnp.zeros((POOL - SLOTS, D), BF16)
    back_in[CAP * 4 : CAP * 5, :] = jnp.zeros((CAP, D), BF16)
    back_in[SLOTS:, :] = jnp.zeros((POOL - SLOTS, D), BF16)
    pl.semaphore_wait(barrier, len(partners))

    def swap_slots(source, target, send, recv, sign):
        copies = []
        for code, (move_x, move_y) in enumerate(TRAVEL):
            if code == 4:
                continue
            rows = pl.ds(code * CAP, CAP)
            copies.append(
                remote(
                    source.at[rows], target.at[rows], send.at[code], recv.at[code],
                    at(sign * move_x, sign * move_y),
                )
            )
        for copy in copies:
            copy.start()
        return copies

    def swap_halo(source, target, send, recv, sign):
        copies = []
        for index, (move_x, move_y, first, size) in enumerate(HALO_BLOCKS):
            rows = pl.ds(first, size)
            copies.append(
                remote(
                    source.at[rows], target.at[rows], send.at[index], recv.at[index],
                    at(sign * move_x, sign * move_y),
                )
            )
        for copy in copies:
            copy.start()
        return copies

    def landed(copies):
        for copy in copies:
            copy.wait_recv()

    everything = []
    migration = swap_slots(outgoing, arrived, mig_s, mig_r, 1)
    everything += migration

    stay_pick = one_hot_lanes(column(jnp.where(from_row == 4.0, aslot_row, -1.0)), ROWS)
    come_pick = one_hot_lanes(column(jnp.where(from_row == 4.0, -1.0, from_row * CAP + aslot_row)), POOL)
    staying = dot(stay_pick, lat[...])
    for index in range(4):
        filled = column(face[index : index + 1, :].astype(F32))
        pick_send[index * 64 : index * 64 + 64, :] = one_hot_lanes(filled, ROWS)
    for index in range(4):
        filled = column(corner[index : index + 1, :].astype(F32))
        pick_send[256 + index * 16 : 272 + index * 16, :] = one_hot_lanes(filled, ROWS)
    count_col[...] = column(as_row(count))

    def build_hits(k, carry):
        row = nbr[pl.ds(k, 1), :].astype(F32)
        high = row >= float(HALF)
        inner = jnp.where(high, row - float(HALF), row)
        hits[k] = one_hot_lanes(column(inner), ROWS)
        upper[k] = column(jnp.where(high, 1.0, 0.0))
        return carry

    lax.fori_loop(0, K, build_hits, 0)

    def build_hits_t(k, carry):
        row = nbr[pl.ds(k, 1), :].astype(F32)
        hits_t[k] = one_hot_rows(jnp.where(row >= float(HALF), row - float(HALF), row), HALF)
        return carry

    for load in loads[9:]:
        load.wait()

    diag = (lax.broadcasted_iota(jnp.int32, (2 * D, 2 * D), 0) // D) == (
        lax.broadcasted_iota(jnp.int32, (2 * D, 2 * D), 1) // D
    )
    ones[...] = jnp.where(diag, 1.0 / D, 0.0).astype(BF16)

    def doubled(weight):
        both = jnp.concatenate([twice(weight), twice(weight)], axis=0)
        return jnp.where(diag, both, 0.0).astype(BF16)

    for layer in range(LAYERS):
        mid = e_hid[layer, 0].astype(F32) * 0.5
        out = e_hid[layer, 1].astype(F32)
        w_mid[layer] = doubled(mid)
        w_out[layer] = doubled(out - jnp.mean(out, axis=1, keepdims=True))
    send_tab[HALF:, :] = jnp.zeros((ROWS - HALF, 2 * D), BF16)

    def bias(layer, index):
        return bia[index, layer : layer + 1, :]

    def gain(layer, index):
        return gai[layer, index : index + 1, :]

    def later_uses():
        lax.fori_loop(0, K, build_hits_t, 0)
        pick_back[...] = jnp.transpose(pick_send[...].astype(F32)).astype(BF16)

    def later_weights():
        for layer in range(LAYERS):
            w_mid_t[layer] = doubled(jnp.transpose(e_hid[layer, 0].astype(F32)) * 0.5)
            w_out_t[layer] = doubled(jnp.transpose(e_hid[layer, 1].astype(F32)) * 0.5)

    landed(migration)
    state[0] = (staying + dot(come_pick, arrived[...])).astype(BF16)

    def forward(layer, meanwhile):
        halo_out[layer] = dot(pick_send[...], state[layer]).astype(BF16)
        halo = swap_halo(halo_out.at[layer], halo_in.at[layer], halo_s.at[layer], halo_r.at[layer], 1)
        everything.extend(halo)
        own = state[layer]
        recv_term[...] = (dot(own, e_in[layer, 0]) + bias(layer, 0)) * 0.5
        w_send = (e_in[layer, 1].astype(F32) * 0.5).astype(BF16)
        own_send = dot(own, w_send).astype(BF16)
        send_tab[0:HALF, 0:D] = own_send[0:HALF]
        send_tab[0 : ROWS - HALF, D:] = own_send[HALF:]
        acc[...] = jnp.zeros((ROWS, D), F32)
        bias_mid = twice(bias(layer, 1)) * 0.5
        bias_out = bias(layer, 2)
        bias_out = twice(bias_out - jnp.mean(bias_out, axis=1, keepdims=True))
        meanwhile()
        landed(halo)
        send_tab[ROWS - HALF : HALF, D:] = dot(halo_in[layer], w_send).astype(BF16)

        def chain(j, first):
            rows = slice(first, first + BLOCK)
            both = [dot(hits[k, rows], send_tab[...]) for k in (j, j + PAIRS)]
            yield
            parts = [
                recv_term[rows] + jnp.where(upper[k, rows] > 0.5, pick[:, D:], pick[:, :D])
                for k, pick in zip((j, j + PAIRS), both)
            ]
            value, slope = half_silu(jnp.concatenate(parts, axis=1))
            value = value.astype(BF16)
            h1s[layer, j, rows] = value
            d1s[layer, j, rows] = slope.astype(BF16)
            product = dot(value, w_mid[layer])
            yield
            value, slope = half_silu(product + bias_mid)
            value = value.astype(BF16)
            h2s[layer, j, rows] = value
            d2s[layer, j, rows] = slope.astype(BF16)
            product = dot(value, w_out[layer])
            yield
            centred = product + bias_out
            variance = dot((centred * centred).astype(BF16), ones[...])
            yield
            scale = lax.rsqrt(variance + 1e-05)
            live = count_col[rows]
            low_slot = jnp.float32(j) if isinstance(j, int) else j.astype(F32)
            mask = jnp.concatenate([live > low_slot, live > low_slot + PAIRS], axis=1)
            scale = jnp.where(mask, scale, 0.0)
            normed = centred * scale
            rss[layer, j, rows] = scale.astype(BF16)
            xhs[layer, j, rows] = normed.astype(BF16)
            acc[rows] += normed[:, :D] + normed[:, D:]

        staggered(chain, FORWARD_PAIRS)
        total = acc[...]
        agg_raw[layer] = total
        total = (total * gain(layer, 0)).astype(BF16)
        agg[layer] = total
        half = (dot(own, n_in[layer, 0]) + dot(total, n_in[layer, 1]) + bias(layer, 3)) * 0.5
        value, slope = half_silu(half)
        value = value.astype(BF16)
        nhs[layer] = value
        d3s[layer] = slope
        normed, scale = layer_norm_parts(dot(value, n_out[layer]) + bias(layer, 4))
        xh2s[layer] = normed
        rs2s[layer] = jnp.broadcast_to(scale, (ROWS, D))
        return (own.astype(F32) + normed * gain(layer, 1)).astype(BF16)

    for layer in range(LAYERS):
        following = forward(layer, (later_uses, later_weights)[layer])
        if layer + 1 < LAYERS:
            state[layer + 1] = following
        else:
            state_o[...] = following

    def put_term(group, index, values):
        refs["terms_" + group][index * D : index * D + D, :] = values.astype(BF16)

    def reduce_start(group):
        terms, arriving = refs["terms_" + group], refs["rs_in_" + group]
        chunk = arriving.shape[1]
        copies = []
        for step in range(1, ny):
            peer = lax.rem(b + step, ny)
            rows = pl.ds(pl.multiple_of(peer * chunk, chunk), chunk)
            sems = (refs["rs_s_" + group].at[step - 1], refs["rs_r_" + group].at[step - 1])
            copies.append(remote(terms.at[rows], arriving.at[step - 1], *sems, (a, peer)))
        for copy in copies:
            copy.start()
        everything.extend(copies)
        return copies

    def exchange_start(group, reducing):
        terms, arriving, summed = refs["terms_" + group], refs["rs_in_" + group], refs["ar_buf_" + group]
        chunk = arriving.shape[1]
        landed(reducing)
        total = terms[pl.ds(pl.multiple_of(b * chunk, chunk), chunk), :].astype(F32)
        for step in range(ny - 1):
            total = total + arriving[step].astype(F32)
        summed[a] = total.astype(BF16)
        out, come = [], []
        for step in range(1, nx):
            peer = lax.rem(a + step, nx)
            source = lax.rem(a + (nx - step), nx)
            sems = (refs["ar_s_" + group].at[step - 1], refs["ar_r_" + group].at[step - 1])
            out.append(remote(summed.at[a], summed.at[a], *sems, (peer, b)))
            come.append(remote(summed.at[source], summed.at[source], *sems, (peer, b)))
        for copy in out:
            copy.start()
        everything.extend(out)
        return come

    def spread_start(group, exchanging):
        summed, final = refs["ar_buf_" + group], refs["final_" + group]
        landed(exchanging)
        total = summed[0].astype(F32)
        for step in range(1, nx):
            total = total + summed[step].astype(F32)
        final[b] = total.astype(BF16)
        out, come = [], []
        for step in range(1, ny):
            peer = lax.rem(b + step, ny)
            source = lax.rem(b + (ny - step), ny)
            sems = (refs["ag_s_" + group].at[step - 1], refs["ag_r_" + group].at[step - 1])
            out.append(remote(final.at[b], final.at[b], *sems, (a, peer)))
            come.append(remote(final.at[source], final.at[source], *sems, (a, peer)))
        for copy in out:
            copy.start()
        everything.extend(out)
        return come

    vectors = []

    def backward(layer, cotangent, before_edges, after_terms):
        own = state[layer]
        normed = xh2s[layer]
        lifted = cotangent * gain(layer, 1)
        grad_gain_node = jnp.sum(cotangent * normed, axis=0, keepdims=True)
        inner = jnp.mean(lifted * normed, axis=1, keepdims=True)
        grad = rs2s[layer] * (lifted - jnp.mean(lifted, axis=1, keepdims=True) - normed * inner)
        grad_b4 = jnp.sum(grad, axis=0, keepdims=True)
        grad = grad.astype(BF16)
        put_term("early", NODE_TERMS[layer] + 2, dot_tn(nhs[layer], grad))
        grad = dot_nt(grad, n_out[layer]) * (d3s[layer] * 0.5)
        grad_b3 = jnp.sum(grad, axis=0, keepdims=True)
        grad = grad.astype(BF16)
        put_term("early", NODE_TERMS[layer], dot_tn(own, grad))
        put_term("early", NODE_TERMS[layer] + 1, dot_tn(agg[layer], grad))
        own_grad = cotangent + dot_nt(grad, n_in[layer, 0])
        grad_agg = dot_nt(grad, n_in[layer, 1])
        grad_gain_edge = jnp.sum(grad_agg * agg_raw[layer], axis=0, keepdims=True)
        lifted = grad_agg * gain(layer, 0)
        dxc[...] = lifted - jnp.mean(lifted, axis=1, keepdims=True)
        g_recv[...] = jnp.zeros((ROWS, D), F32)
        dsend[...] = jnp.zeros((HALF, 2 * D), F32)
        dw_out[...] = jnp.zeros((D, D), F32)
        dw_mid[...] = jnp.zeros((D, D), F32)
        db_out[...] = jnp.zeros((8, 2 * D), F32)
        db_mid[...] = jnp.zeros((8, 2 * D), F32)
        before_edges()

        def chain(j, first):
            rows = slice(first, first + BLOCK)
            lift = twice(dxc[rows])
            unit = xhs[layer, j, rows].astype(F32)
            shared = dot((lift * unit).astype(BF16), ones[...])
            yield
            grad = rss[layer, j, rows].astype(F32) * (lift - unit * shared)
            db_out[...] += partial_sums(grad)
            grad = grad.astype(BF16)
            product = dot(grad, w_out_t[layer])
            hidden = h2s[layer, j, rows]
            dw_out[...] += dot_tn(hidden[:, :D], grad[:, :D]) + dot_tn(hidden[:, D:], grad[:, D:])
            yield
            grad = product * d2s[layer, j, rows].astype(F32)
            db_mid[...] += partial_sums(grad)
            grad = grad.astype(BF16)
            product = dot(grad, w_mid_t[layer])
            hidden = h1s[layer, j, rows]
            dw_mid[...] += dot_tn(hidden[:, :D], grad[:, :D]) + dot_tn(hidden[:, D:], grad[:, D:])
            yield
            grad = product * d1s[layer, j, rows].astype(F32)
            g_recv[rows] += grad[:, :D] + grad[:, D:]
            scattered = None
            for part in range(2):
                k = j + part * PAIRS
                piece = grad[:, part * D : part * D + D]
                high = upper[k, rows] > 0.5
                split = jnp.concatenate([jnp.where(high, 0.0, piece), jnp.where(high, piece, 0.0)], axis=1)
                added = dot(hits_t[k, :, rows], split.astype(BF16))
                scattered = added if scattered is None else scattered + added
            dsend[...] += scattered

        staggered(chain, BACKWARD_PAIRS)
        send_grad = dsend[...].astype(BF16)
        low = send_grad[:, :D]
        high_own = send_grad[: ROWS - HALF, D:]
        high_halo = send_grad[ROWS - HALF :, D:]
        ret_out[layer] = dot_nt(high_halo, e_in[layer, 1]).astype(BF16)
        returning = swap_halo(ret_out.at[layer], ret_in.at[layer], ret_s.at[layer], ret_r.at[layer], -1)
        everything.extend(returning)
        send_own = jnp.concatenate([low, high_own], axis=0)
        term = dot_tn(own, send_own) + dot_tn(halo_in[layer], high_halo)
        group = EDGE_GROUPS[layer]
        put_term(group, 1, term)
        grad = g_recv[...]
        grad_b0 = jnp.sum(grad, axis=0, keepdims=True)
        grad = grad.astype(BF16)
        put_term(group, 0, dot_tn(own, grad))
        put_term(group, 2, dw_mid[...])
        put_term(group, 3, dw_out[...])
        total_mid = jnp.sum(db_mid[...], axis=0, keepdims=True)
        total_out = jnp.sum(db_out[...], axis=0, keepdims=True)
        vectors.extend([
            grad_b0,
            total_mid[:, :D] + total_mid[:, D:],
            total_out[:, :D] + total_out[:, D:],
            grad_b3,
            grad_b4,
            grad_gain_edge,
            grad_gain_node,
        ])
        after_terms()
        own_grad = own_grad + dot_nt(grad, e_in[layer, 0]) + dot_nt(send_own, e_in[layer, 1])
        landed(returning)
        own_grad = own_grad + dot(pick_back[...], ret_in[layer])
        return own_grad.astype(BF16)

    sums = {}

    def early_start():
        sums["early"] = reduce_start("early")

    def late_start():
        terms = refs["terms_late"]
        terms[LATE_VECTORS:, :] = jnp.zeros((LATE_ROWS - LATE_VECTORS, D), BF16)
        stacked = jnp.concatenate(vectors + [jnp.zeros((2, D), F32)], axis=0)
        terms[LATE_VECTORS : LATE_VECTORS + 16, :] = stacked.astype(BF16)
        sums["late"] = reduce_start("late")
        sums["early"] = exchange_start("early", sums["early"])

    rounded = backward(1, gout[...].astype(F32), lambda: None, lambda: None)
    rounded = backward(0, rounded.astype(F32), early_start, late_start)

    back_target = jnp.where(from_row == 4.0, -1.0, from_row * CAP + aslot_row)
    back_out[...] = dot(one_hot_rows(back_target, SLOTS), rounded).astype(BF16)
    going_back = swap_slots(back_out, back_in, back_s, back_r, -1)
    everything += going_back
    sums["late"] = exchange_start("late", sums["late"])
    stay_pick = one_hot_lanes(column(jnp.where(to_row == 4.0, slot_row, -1.0)), ROWS)
    come_pick = one_hot_lanes(column(out_target), POOL)
    staying = dot(stay_pick, rounded)
    sums["early"] = spread_start("early", sums["early"])
    landed(going_back)
    glat_o[...] = (staying + dot(come_pick, back_in[...])).astype(BF16)
    sums["late"] = spread_start("late", sums["late"])
    landed(sums["early"])
    early_o[...] = refs["final_early"][...].reshape(EARLY_ROWS, D)
    landed(sums["late"])
    late_o[...] = refs["final_late"][...].reshape(LATE_ROWS, D)
    for copy in everything:
        copy.wait_send()


def unpack(state, grad_latent, early, late, state_o, glat_o, gein_o, gehid_o, gnin_o, gnout_o, gbia_o, ggai_o):
    state_o[...] = state[...]
    glat_o[...] = grad_latent[...]
    sums = dict(early=early, late=late)

    def matrix(group, index):
        return sums[group][index * D : index * D + D, :].astype(F32)

    for layer in range(LAYERS):
        group, node = EDGE_GROUPS[layer], NODE_TERMS[layer]
        for index in range(2):
            gein_o[layer, index] = matrix(group, index)
            gehid_o[layer, index] = matrix(group, index + 2)
            gnin_o[layer, index] = matrix("early", node + index)
        gnout_o[layer] = matrix("early", node + 2)
    vectors = late[LATE_VECTORS : LATE_VECTORS + 16, :].astype(F32)
    for layer in range(LAYERS):
        first = 7 * (LAYERS - 1 - layer)
        gbia_o[:, layer] = vectors[first : first + 5]
        ggai_o[layer] = vectors[first + 5 : first + 7]


def shards(
    latent, move_to, move_slot, arrive_from, arrive_slot, neighbours, valid_count, face_send, corner_send,
    edge_in, edge_hid, node_in, node_out, biases, gains, grad_out,
):
    nx, ny = lax.axis_size("bx"), lax.axis_size("by")
    vmem = pl.BlockSpec(memory_space=pltpu.VMEM)
    shape = jax.ShapeDtypeStruct
    saved = pltpu.VMEM((LAYERS, PAIRS, ROWS, 2 * D), BF16)
    node = pltpu.VMEM((LAYERS, ROWS, D), F32)
    node_bf = pltpu.VMEM((LAYERS, ROWS, D), BF16)
    wide = pltpu.VMEM((LAYERS, 2 * D, 2 * D), BF16)
    dma = pltpu.SemaphoreType.DMA
    scratch = dict(
        outgoing=pltpu.VMEM((SLOTS, D), BF16),
        arrived=pltpu.VMEM((POOL, D), BF16),
        halo_out=pltpu.VMEM((LAYERS, HALO, D), BF16),
        halo_in=pltpu.VMEM((LAYERS, HALO, D), BF16),
        ret_out=pltpu.VMEM((LAYERS, HALO, D), BF16),
        ret_in=pltpu.VMEM((LAYERS, HALO, D), BF16),
        back_out=pltpu.VMEM((SLOTS, D), BF16),
        back_in=pltpu.VMEM((POOL, D), BF16),
        pick_send=pltpu.VMEM((HALO, ROWS), BF16),
        pick_back=pltpu.VMEM((ROWS, HALO), BF16),
        hits=pltpu.VMEM((K, ROWS, ROWS), BF16),
        hits_t=pltpu.VMEM((K, HALF, ROWS), BF16),
        upper=pltpu.VMEM((K, ROWS, D), F32),
        count_col=pltpu.VMEM((ROWS, D), F32),
        state=node_bf,
        recv_term=pltpu.VMEM((ROWS, D), F32),
        send_tab=pltpu.VMEM((ROWS, 2 * D), BF16),
        w_mid=wide,
        w_out=wide,
        w_mid_t=wide,
        w_out_t=wide,
        ones=pltpu.VMEM((2 * D, 2 * D), BF16),
        h1s=saved,
        h2s=saved,
        d1s=saved,
        d2s=saved,
        xhs=saved,
        rss=saved,
        acc=pltpu.VMEM((ROWS, D), F32),
        agg=node_bf,
        nhs=node_bf,
        d3s=node,
        xh2s=node,
        rs2s=node,
        dxc=pltpu.VMEM((ROWS, D), F32),
        g_recv=pltpu.VMEM((ROWS, D), F32),
        agg_raw=node,
        dsend=pltpu.VMEM((HALF, 2 * D), F32),
        dw_out=pltpu.VMEM((D, D), F32),
        dw_mid=pltpu.VMEM((D, D), F32),
        db_out=pltpu.VMEM((8, 2 * D), F32),
        db_mid=pltpu.VMEM((8, 2 * D), F32),
        mig_s=dma((CODES,)),
        mig_r=dma((CODES,)),
        halo_s=dma((LAYERS, 8)),
        halo_r=dma((LAYERS, 8)),
        ret_s=dma((LAYERS, 8)),
        ret_r=dma((LAYERS, 8)),
        back_s=dma((CODES,)),
        back_r=dma((CODES,)),
        load_s=dma((16,)),
    )
    for group, total in (("early", EARLY_ROWS), ("late", LATE_ROWS)):
        chunk = total // ny
        scratch["terms_" + group] = pltpu.VMEM((total, D), BF16)
        scratch["rs_in_" + group] = pltpu.VMEM((ny - 1, chunk, D), BF16)
        scratch["ar_buf_" + group] = pltpu.VMEM((nx, chunk, D), BF16)
        scratch["final_" + group] = pltpu.VMEM((ny, chunk, D), BF16)
        for stage, partners in (("rs", ny), ("ar", nx), ("ag", ny)):
            scratch[f"{stage}_s_{group}"] = dma((partners - 1,))
            scratch[f"{stage}_r_{group}"] = dma((partners - 1,))

    def row(values):
        return values.reshape(1, ROWS)

    arguments = (
        latent, row(move_to), row(move_slot), row(arrive_from), row(arrive_slot),
        neighbours.T, row(valid_count), face_send.reshape(4, -1), corner_send.reshape(4, -1),
        edge_in, edge_hid, node_in, node_out, biases.transpose(1, 0, 2), gains, grad_out,
    )
    for name, value in zip(ARGUMENTS, arguments):
        scratch[name] = pltpu.VMEM(value.shape, value.dtype)
    names = ["arg_" + name for name in ARGUMENTS] + list(RESULTS) + list(scratch)
    state, grad_latent, early, late = pl.pallas_call(
        functools.partial(kernel, nx, ny, names),
        out_shape=(
            shape((ROWS, D), BF16),
            shape((ROWS, D), BF16),
            shape((EARLY_ROWS, D), BF16),
            shape((LATE_ROWS, D), BF16),
        ),
        in_specs=[pl.BlockSpec(memory_space=pl.ANY)] * len(ARGUMENTS),
        out_specs=(vmem,) * len(RESULTS),
        scratch_shapes=list(scratch.values()),
        compiler_params=pltpu.CompilerParams(
            collective_id=0, has_side_effects=True, vmem_limit_bytes=60 * 1024 * 1024
        ),
        name="evolve",
    )(*arguments)
    outputs = pl.pallas_call(
        unpack,
        out_shape=(
            shape((ROWS, D), BF16),
            shape((ROWS, D), BF16),
            shape((LAYERS, 2, D, D), F32),
            shape((LAYERS, 2, D, D), F32),
            shape((LAYERS, 2, D, D), F32),
            shape((LAYERS, D, D), F32),
            shape((5, LAYERS, D), F32),
            shape((LAYERS, 2, D), F32),
        ),
        in_specs=[vmem] * 4,
        out_specs=(vmem,) * 8,
        name="unpack",
    )(state, grad_latent, early, late)
    return *outputs[:6], outputs[6].transpose(1, 0, 2), outputs[7]


def solution(mesh):
    both = ("bx", "by")
    rows, wide, grid = P(both), P(both, None), P("bx", "by", None, None)
    return jax.shard_map(
        shards,
        mesh=mesh,
        in_specs=(wide, rows, rows, rows, rows, wide, rows, grid, grid, P(), P(), P(), P(), P(), P(), wide),
        out_specs=(wide, wide, P(), P(), P(), P(), P(), P()),
        check_vma=False,
    )
```

```python
import functools

import jax
import jax.numpy as jnp
from jax import lax
from jax.experimental import pallas as pl
from jax.experimental.pallas import tpu as pltpu
from jax.sharding import PartitionSpec as P

LAYERS = 2
CAP = 32
D = 128
K = 16
PAIRS = K // 2
ROWS = 512
HALF = 256
HALO_HALF = 160
PLACES = HALF + HALO_HALF
HALO = 320
CODES = 9
SLOTS = CODES * CAP
POOL = 384
EARLY_ROWS = 1280
LATE_ROWS = 768
LATE_VECTORS = 512
BLOCK = 512
FORWARD_PAIRS = 4
BACKWARD_PAIRS = 4
F32 = jnp.float32
BF16 = jnp.bfloat16
MESH = pl.DeviceIdType.MESH
TRAVEL = tuple((code // 3 - 1, code % 3 - 1) for code in range(CODES))
HALO_BLOCKS = (
    (1, 0, 0, 64),
    (-1, 0, 64, 64),
    (0, 1, 128, 64),
    (0, -1, 192, 64),
    (1, 1, 256, 16),
    (1, -1, 272, 16),
    (-1, 1, 288, 16),
    (-1, -1, 304, 16),
)

ARGUMENTS = (
    "lat", "move_to", "move_slot", "arrive_from", "arrive_slot", "nbr", "count", "face", "corner",
    "e_in", "e_hid", "n_in", "n_out", "bia", "gai", "gout",
)
RESULTS = ("state_o", "glat_o", "early_o", "late_o")
SCRATCH = (
    "outgoing", "arrived", "halo_out", "halo_in", "ret_out", "ret_in", "back_out", "back_in",
    "pick_send", "pick_back", "hits", "hits_t", "upper", "count_col", "state", "recv_term",
    "own_tab", "halo_tab", "before", "w_mid", "w_out", "w_mid_t", "w_out_t", "ones", "h1s", "h2s", "d1s", "d2s", "xhs",
    "rss", "acc", "agg", "nhs", "d3s", "xh2s", "rs2s", "dxc", "g_recv", "agg_raw", "dsend",
    "dw_out", "dw_mid", "db_out", "db_mid", "mig_s", "mig_r", "halo_s", "halo_r", "ret_s", "ret_r",
    "back_s", "back_r",
)
EDGE_GROUPS = ("late", "early")
NODE_TERMS = (7, 4)


def dot(a, b):
    return jnp.dot(a, b, preferred_element_type=F32)


def dot_nt(a, b):
    return lax.dot_general(a, b, (((1,), (1,)), ((), ())), preferred_element_type=F32)


def dot_tn(a, b):
    return lax.dot_general(a, b, (((0,), (0,)), ((), ())), preferred_element_type=F32)


def column(row):
    return jnp.transpose(jnp.broadcast_to(row, (D, row.shape[1])))


def one_hot_lanes(filled, width):
    lane = lax.broadcasted_iota(jnp.int32, filled.shape, 1).astype(F32)
    pieces = [
        jnp.where(filled == lane + float(start), 1.0, 0.0).astype(BF16) for start in range(0, width, D)
    ]
    return jnp.concatenate(pieces, axis=1)


def one_hot_rows(row, height):
    index = lax.broadcasted_iota(jnp.int32, (height, row.shape[1]), 0).astype(F32)
    return jnp.where(index == row, 1.0, 0.0).astype(BF16)


def twice(values):
    return jnp.concatenate([values, values], axis=1)


def partial_sums(values):
    return jnp.sum(values.reshape(values.shape[0] // 8, 8, values.shape[1]), axis=0)


def staggered(chain, pairs):
    def body(group, carry):
        waiting = [
            chain(group * pairs + pair, first) for pair in range(pairs) for first in range(0, ROWS, BLOCK)
        ]
        running = []
        while waiting or running:
            if waiting:
                running.append(waiting.pop(0))
            running = [one for one in running if next(one, True) is None]
        return carry

    lax.fori_loop(0, PAIRS // pairs, body, 0)


def layer_norm_parts(values):
    centred = values - jnp.mean(values, axis=1, keepdims=True)
    scale = lax.rsqrt(jnp.mean(centred * centred, axis=1, keepdims=True) + 1e-05)
    return centred * scale, scale


def half_silu(half):
    wave = jnp.tanh(half)
    gate = 1.0 + wave
    value = half * gate
    return value, gate + value * (1.0 - wave)


def kernel(
    nx, ny, names, *refs
):
    refs = dict(zip(names, refs))
    arguments = [(refs["arg_" + name], refs[name]) for name in ARGUMENTS]
    (
        lat, move_to, move_slot, arrive_from, arrive_slot, nbr, count, face, corner,
        e_in, e_hid, n_in, n_out, bia, gai, gout,
    ) = (local for _, local in arguments)
    (
        outgoing, arrived, halo_out, halo_in, ret_out, ret_in, back_out, back_in,
        pick_send, pick_back, hits, hits_t, upper, count_col,
        state, recv_term, own_tab, halo_tab, before, w_mid, w_out, w_mid_t, w_out_t, ones,
        h1s, h2s, d1s, d2s, xhs, rss, acc, agg, nhs, d3s, xh2s, rs2s,
        dxc, g_recv, agg_raw, dsend, dw_out, dw_mid, db_out, db_mid,
        mig_s, mig_r, halo_s, halo_r, ret_s, ret_r, back_s, back_r,
    ) = (refs[name] for name in SCRATCH)
    a = lax.axis_index("bx")
    b = lax.axis_index("by")

    def at(move_x, move_y):
        return (lax.rem(a + (move_x + nx), nx), lax.rem(b + (move_y + ny), ny))

    def remote(src, dst, send, recv, target):
        return pltpu.make_async_remote_copy(
            src_ref=src, dst_ref=dst, send_sem=send, recv_sem=recv, device_id=target, device_id_type=MESH
        )

    barrier = pltpu.get_barrier_semaphore()
    partners = [(0, step) for step in range(1, ny)] + [(step, 0) for step in range(1, nx)]
    partners += [(1, 1), (1, -1), (-1, 1), (-1, -1)]
    for move_x, move_y in partners:
        pl.semaphore_signal(barrier, inc=1, device_id=at(move_x, move_y), device_id_type=MESH)

    loads = [
        pltpu.make_async_copy(there, here, refs["load_s"].at[index])
        for index, (there, here) in enumerate(arguments)
    ]
    for load in loads:
        load.start()
    for load in loads[:9]:
        load.wait()

    def as_row(ref):
        return ref[...].astype(F32)

    to_row, slot_row = as_row(move_to), as_row(move_slot)
    from_row, aslot_row = as_row(arrive_from), as_row(arrive_slot)
    out_target = jnp.where(to_row == 4.0, -1.0, to_row * CAP + slot_row)
    outgoing[...] = dot(one_hot_rows(out_target, SLOTS), lat[...]).astype(BF16)
    arrived[CAP * 4 : CAP * 5, :] = jnp.zeros((CAP, D), BF16)
    arrived[SLOTS:, :] = jnp.zeros((POOL - SLOTS, D), BF16)
    back_in[CAP * 4 : CAP * 5, :] = jnp.zeros((CAP, D), BF16)
    back_in[SLOTS:, :] = jnp.zeros((POOL - SLOTS, D), BF16)
    pl.semaphore_wait(barrier, len(partners))

    def swap_slots(source, target, send, recv, sign):
        copies = []
        for code, (move_x, move_y) in enumerate(TRAVEL):
            if code == 4:
                continue
            rows = pl.ds(code * CAP, CAP)
            copies.append(
                remote(
                    source.at[rows], target.at[rows], send.at[code], recv.at[code],
                    at(sign * move_x, sign * move_y),
                )
            )
        for copy in copies:
            copy.start()
        return copies

    def swap_halo(source, target, send, recv, sign):
        copies = []
        for index, (move_x, move_y, first, size) in enumerate(HALO_BLOCKS):
            rows = pl.ds(first, size)
            copies.append(
                remote(
                    source.at[rows], target.at[rows], send.at[index], recv.at[index],
                    at(sign * move_x, sign * move_y),
                )
            )
        for copy in copies:
            copy.start()
        return copies

    def landed(copies):
        for copy in copies:
            copy.wait_recv()

    everything = []
    stored = []

    def put_result(local, result):
        copy = pltpu.make_async_copy(refs[local], refs[result], refs["store_s"].at[len(stored)])
        copy.start()
        stored.append(copy)

    migration = swap_slots(outgoing, arrived, mig_s, mig_r, 1)
    everything += migration

    stay_pick = one_hot_lanes(column(jnp.where(from_row == 4.0, aslot_row, -1.0)), ROWS)
    come_pick = one_hot_lanes(column(jnp.where(from_row == 4.0, -1.0, from_row * CAP + aslot_row)), POOL)
    staying = dot(stay_pick, lat[...])
    for index in range(4):
        filled = column(face[index : index + 1, :].astype(F32))
        pick_send[index * 64 : index * 64 + 64, :] = one_hot_lanes(filled, ROWS)
    for index in range(4):
        filled = column(corner[index : index + 1, :].astype(F32))
        pick_send[256 + index * 16 : 272 + index * 16, :] = one_hot_lanes(filled, ROWS)
    count_col[...] = column(as_row(count))

    def placed(row):
        halo = row - float(ROWS)
        own_high = row >= float(HALF)
        halo_high = halo >= float(HALO_HALF)
        own_place = jnp.where(own_high, row - float(HALF), row)
        halo_place = jnp.where(halo_high, halo - float(HALO_HALF), halo) + float(HALF)
        own = row < float(ROWS)
        high = jnp.where(own, jnp.where(own_high, 1.0, 0.0), jnp.where(halo_high, 1.0, 0.0))
        return jnp.where(own, own_place, halo_place), high

    def build_hits(k, carry):
        place, high = placed(nbr[pl.ds(k, 1), :].astype(F32))
        hits[k] = one_hot_lanes(column(place), ROWS)
        upper[k] = column(high)
        return carry

    lax.fori_loop(0, K, build_hits, 0)

    def build_hits_t(k, carry):
        hits_t[k] = one_hot_rows(placed(nbr[pl.ds(k, 1), :].astype(F32))[0], PLACES)
        return carry

    for load in loads[9:]:
        load.wait()

    diag = (lax.broadcasted_iota(jnp.int32, (2 * D, 2 * D), 0) // D) == (
        lax.broadcasted_iota(jnp.int32, (2 * D, 2 * D), 1) // D
    )
    ones[...] = jnp.where(diag, 1.0 / D, 0.0).astype(BF16)

    def doubled(weight):
        both = jnp.concatenate([twice(weight), twice(weight)], axis=0)
        return jnp.where(diag, both, 0.0).astype(BF16)

    for layer in range(LAYERS):
        mid = e_hid[layer, 0].astype(F32) * 0.5
        out = e_hid[layer, 1].astype(F32)
        w_mid[layer] = doubled(mid)
        w_out[layer] = doubled(out - jnp.mean(out, axis=1, keepdims=True))
    halo_tab[HALO_HALF:, :] = jnp.zeros((HALF - HALO_HALF, 2 * D), BF16)

    def bias(layer, index):
        return bia[index, layer : layer + 1, :]

    def gain(layer, index):
        return gai[layer, index : index + 1, :]

    def later_uses():
        lax.fori_loop(0, K, build_hits_t, 0)
        pick_back[...] = jnp.transpose(pick_send[...].astype(F32)).astype(BF16)

    def later_weights():
        for layer in range(LAYERS):
            w_mid_t[layer] = doubled(jnp.transpose(e_hid[layer, 0].astype(F32)) * 0.5)
            w_out_t[layer] = doubled(jnp.transpose(e_hid[layer, 1].astype(F32)) * 0.5)

    landed(migration)
    state[0] = (staying + dot(come_pick, arrived[...])).astype(BF16)

    def forward(layer, meanwhile):
        halo_out[layer] = dot(pick_send[...], state[layer]).astype(BF16)
        halo = swap_halo(halo_out.at[layer], halo_in.at[layer], halo_s.at[layer], halo_r.at[layer], 1)
        everything.extend(halo)
        own = state[layer]
        recv_term[...] = (dot(own, e_in[layer, 0]) + bias(layer, 0)) * 0.5
        w_send = (e_in[layer, 1].astype(F32) * 0.5).astype(BF16)
        own_send = dot(own, w_send).astype(BF16)
        own_tab[:, :D] = own_send[:HALF]
        own_tab[:, D:] = own_send[HALF:]
        acc[...] = jnp.zeros((ROWS, D), F32)
        bias_mid = twice(bias(layer, 1)) * 0.5
        bias_out = bias(layer, 2)
        bias_out = twice(bias_out - jnp.mean(bias_out, axis=1, keepdims=True))
        meanwhile()

        def own_chain(j, first):
            rows = slice(first, first + BLOCK)
            slots = (j, j + PAIRS)
            both = [dot(hits[k, rows, :HALF], own_tab[...]) for k in slots]
            yield
            for k, pick in zip(slots, both):
                before[k, rows] = recv_term[rows] + jnp.where(upper[k, rows] > 0.5, pick[:, D:], pick[:, :D])

        staggered(own_chain, 4)
        landed(halo)
        halo_send = dot(halo_in[layer], w_send).astype(BF16)
        halo_tab[:HALO_HALF, :D] = halo_send[:HALO_HALF]
        halo_tab[:HALO_HALF, D:] = halo_send[HALO_HALF:]

        def chain(j, first):
            rows = slice(first, first + BLOCK)
            both = [dot(hits[k, rows, HALF:], halo_tab[...]) for k in (j, j + PAIRS)]
            yield
            parts = [
                before[k, rows] + jnp.where(upper[k, rows] > 0.5, pick[:, D:], pick[:, :D])
                for k, pick in zip((j, j + PAIRS), both)
            ]
            value, slope = half_silu(jnp.concatenate(parts, axis=1))
            value = value.astype(BF16)
            h1s[layer, j, rows] = value
            d1s[layer, j, rows] = slope.astype(BF16)
            product = dot(value, w_mid[layer])
            yield
            value, slope = half_silu(product + bias_mid)
            value = value.astype(BF16)
            h2s[layer, j, rows] = value
            d2s[layer, j, rows] = slope.astype(BF16)
            product = dot(value, w_out[layer])
            yield
            centred = product + bias_out
            variance = dot((centred * centred).astype(BF16), ones[...])
            yield
            scale = lax.rsqrt(variance + 1e-05)
            live = count_col[rows]
            low_slot = jnp.float32(j) if isinstance(j, int) else j.astype(F32)
            mask = jnp.concatenate([live > low_slot, live > low_slot + PAIRS], axis=1)
            scale = jnp.where(mask, scale, 0.0)
            normed = centred * scale
            rss[layer, j, rows] = scale.astype(BF16)
            xhs[layer, j, rows] = normed.astype(BF16)
            acc[rows] += normed[:, :D] + normed[:, D:]

        staggered(chain, FORWARD_PAIRS)
        total = acc[...]
        agg_raw[layer] = total
        total = (total * gain(layer, 0)).astype(BF16)
        agg[layer] = total
        half = (dot(own, n_in[layer, 0]) + dot(total, n_in[layer, 1]) + bias(layer, 3)) * 0.5
        value, slope = half_silu(half)
        value = value.astype(BF16)
        nhs[layer] = value
        d3s[layer] = slope
        normed, scale = layer_norm_parts(dot(value, n_out[layer]) + bias(layer, 4))
        xh2s[layer] = normed
        rs2s[layer] = jnp.broadcast_to(scale, (ROWS, D))
        return (own.astype(F32) + normed * gain(layer, 1)).astype(BF16)

    for layer in range(LAYERS):
        following = forward(layer, (later_uses, later_weights)[layer])
        if layer + 1 < LAYERS:
            state[layer + 1] = following
        else:
            refs["state_v"][...] = following
            put_result("state_v", "state_o")

    def put_term(group, index, values):
        refs["terms_" + group][index * D : index * D + D, :] = values.astype(BF16)

    def reduce_start(group):
        terms, arriving = refs["terms_" + group], refs["rs_in_" + group]
        chunk = arriving.shape[1]
        copies = []
        for step in range(1, ny):
            peer = lax.rem(b + step, ny)
            rows = pl.ds(pl.multiple_of(peer * chunk, chunk), chunk)
            sems = (refs["rs_s_" + group].at[step - 1], refs["rs_r_" + group].at[step - 1])
            copies.append(remote(terms.at[rows], arriving.at[step - 1], *sems, (a, peer)))
        for copy in copies:
            copy.start()
        everything.extend(copies)
        return copies

    def exchange_start(group, reducing):
        terms, arriving, summed = refs["terms_" + group], refs["rs_in_" + group], refs["ar_buf_" + group]
        chunk = arriving.shape[1]
        landed(reducing)
        total = terms[pl.ds(pl.multiple_of(b * chunk, chunk), chunk), :].astype(F32)
        for step in range(ny - 1):
            total = total + arriving[step].astype(F32)
        summed[a] = total.astype(BF16)
        out, come = [], []
        for step in range(1, nx):
            peer = lax.rem(a + step, nx)
            source = lax.rem(a + (nx - step), nx)
            sems = (refs["ar_s_" + group].at[step - 1], refs["ar_r_" + group].at[step - 1])
            out.append(remote(summed.at[a], summed.at[a], *sems, (peer, b)))
            come.append(remote(summed.at[source], summed.at[source], *sems, (peer, b)))
        for copy in out:
            copy.start()
        everything.extend(out)
        return come

    def spread_start(group, exchanging):
        summed, final = refs["ar_buf_" + group], refs["final_" + group]
        landed(exchanging)
        total = summed[0].astype(F32)
        for step in range(1, nx):
            total = total + summed[step].astype(F32)
        final[b] = total.astype(BF16)
        out, come = [], []
        for step in range(1, ny):
            peer = lax.rem(b + step, ny)
            source = lax.rem(b + (ny - step), ny)
            sems = (refs["ag_s_" + group].at[step - 1], refs["ag_r_" + group].at[step - 1])
            out.append(remote(final.at[b], final.at[b], *sems, (a, peer)))
            come.append(remote(final.at[source], final.at[source], *sems, (a, peer)))
        for copy in out:
            copy.start()
        everything.extend(out)
        return come

    vectors = []

    def backward(layer, cotangent, before_edges, after_terms):
        own = state[layer]
        normed = xh2s[layer]
        lifted = cotangent * gain(layer, 1)
        grad_gain_node = jnp.sum(cotangent * normed, axis=0, keepdims=True)
        inner = jnp.mean(lifted * normed, axis=1, keepdims=True)
        grad = rs2s[layer] * (lifted - jnp.mean(lifted, axis=1, keepdims=True) - normed * inner)
        grad_b4 = jnp.sum(grad, axis=0, keepdims=True)
        grad = grad.astype(BF16)
        put_term("early", NODE_TERMS[layer] + 2, dot_tn(nhs[layer], grad))
        grad = dot_nt(grad, n_out[layer]) * (d3s[layer] * 0.5)
        grad_b3 = jnp.sum(grad, axis=0, keepdims=True)
        grad = grad.astype(BF16)
        put_term("early", NODE_TERMS[layer], dot_tn(own, grad))
        put_term("early", NODE_TERMS[layer] + 1, dot_tn(agg[layer], grad))
        own_grad = cotangent + dot_nt(grad, n_in[layer, 0])
        grad_agg = dot_nt(grad, n_in[layer, 1])
        grad_gain_edge = jnp.sum(grad_agg * agg_raw[layer], axis=0, keepdims=True)
        lifted = grad_agg * gain(layer, 0)
        dxc[...] = lifted - jnp.mean(lifted, axis=1, keepdims=True)
        g_recv[...] = jnp.zeros((ROWS, D), F32)
        dsend[...] = jnp.zeros((PLACES, 2 * D), F32)
        dw_out[...] = jnp.zeros((D, D), F32)
        dw_mid[...] = jnp.zeros((D, D), F32)
        db_out[...] = jnp.zeros((8, 2 * D), F32)
        db_mid[...] = jnp.zeros((8, 2 * D), F32)
        before_edges()

        later = layer == LAYERS - 1
        lowest = HALF if later else 0

        def add_hidden(total, hidden, grad):
            total[...] += dot_tn(hidden[:, :D], grad[:, :D]) + dot_tn(hidden[:, D:], grad[:, D:])

        def chain(j, first):
            rows = slice(first, first + BLOCK)
            lift = twice(dxc[rows])
            unit = xhs[layer, j, rows].astype(F32)
            shared = dot((lift * unit).astype(BF16), ones[...])
            yield
            grad = rss[layer, j, rows].astype(F32) * (lift - unit * shared)
            db_out[...] += partial_sums(grad)
            grad = grad.astype(BF16)
            product = dot(grad, w_out_t[layer])
            if later:
                hits[j, rows, HALF:] = grad
            else:
                add_hidden(dw_out, h2s[layer, j, rows], grad)
            yield
            grad = product * d2s[layer, j, rows].astype(F32)
            db_mid[...] += partial_sums(grad)
            grad = grad.astype(BF16)
            product = dot(grad, w_mid_t[layer])
            if later:
                hits[j + PAIRS, rows, HALF:] = grad
            else:
                add_hidden(dw_mid, h1s[layer, j, rows], grad)
            yield
            grad = product * d1s[layer, j, rows].astype(F32)
            g_recv[rows] += grad[:, :D] + grad[:, D:]
            scattered = None
            for part in range(2):
                k = j + part * PAIRS
                piece = grad[:, part * D : part * D + D]
                high = upper[k, rows] > 0.5
                split = jnp.concatenate([jnp.where(high, 0.0, piece), jnp.where(high, piece, 0.0)], axis=1)
                split = split.astype(BF16)
                if later:
                    hits[k, rows, :HALF] = split
                added = dot(hits_t[k, lowest:, rows], split)
                scattered = added if scattered is None else scattered + added
            dsend[lowest:] += scattered

        staggered(chain, BACKWARD_PAIRS)
        halo_grad = dsend[HALF:].astype(BF16)
        halo_grad = jnp.concatenate([halo_grad[:, :D], halo_grad[:, D:]], axis=0)
        ret_out[layer] = dot_nt(halo_grad, e_in[layer, 1]).astype(BF16)
        returning = swap_halo(ret_out.at[layer], ret_in.at[layer], ret_s.at[layer], ret_r.at[layer], -1)
        everything.extend(returning)
        if later:

            def rest(j, first):
                rows = slice(first, first + BLOCK)
                dsend[:HALF] += sum(dot(hits_t[k, :HALF, rows], hits[k, rows, :HALF]) for k in (j, j + PAIRS))
                add_hidden(dw_out, h2s[layer, j, rows], hits[j, rows, HALF:])
                add_hidden(dw_mid, h1s[layer, j, rows], hits[j + PAIRS, rows, HALF:])
                yield

            staggered(rest, 2)
        send_own = dsend[:HALF].astype(BF16)
        send_own = jnp.concatenate([send_own[:, :D], send_own[:, D:]], axis=0)
        term = dot_tn(own, send_own) + dot_tn(halo_in[layer], halo_grad)
        group = EDGE_GROUPS[layer]
        put_term(group, 1, term)
        grad = g_recv[...]
        grad_b0 = jnp.sum(grad, axis=0, keepdims=True)
        grad = grad.astype(BF16)
        put_term(group, 0, dot_tn(own, grad))
        put_term(group, 2, dw_mid[...])
        put_term(group, 3, dw_out[...])
        total_mid = jnp.sum(db_mid[...], axis=0, keepdims=True)
        total_out = jnp.sum(db_out[...], axis=0, keepdims=True)
        vectors.extend([
            grad_b0,
            total_mid[:, :D] + total_mid[:, D:],
            total_out[:, :D] + total_out[:, D:],
            grad_b3,
            grad_b4,
            grad_gain_edge,
            grad_gain_node,
        ])
        after_terms()
        own_grad = own_grad + dot_nt(grad, e_in[layer, 0]) + dot_nt(send_own, e_in[layer, 1])
        landed(returning)
        own_grad = own_grad + dot(pick_back[...], ret_in[layer])
        return own_grad.astype(BF16)

    sums = {}

    def early_start():
        sums["early"] = reduce_start("early")

    def late_start():
        terms = refs["terms_late"]
        terms[LATE_VECTORS:, :] = jnp.zeros((LATE_ROWS - LATE_VECTORS, D), BF16)
        stacked = jnp.concatenate(vectors + [jnp.zeros((2, D), F32)], axis=0)
        terms[LATE_VECTORS : LATE_VECTORS + 16, :] = stacked.astype(BF16)
        sums["late"] = reduce_start("late")
        sums["early"] = exchange_start("early", sums["early"])

    rounded = backward(1, gout[...].astype(F32), lambda: None, lambda: None)
    rounded = backward(0, rounded.astype(F32), early_start, late_start)

    back_target = jnp.where(from_row == 4.0, -1.0, from_row * CAP + aslot_row)
    back_out[...] = dot(one_hot_rows(back_target, SLOTS), rounded).astype(BF16)
    going_back = swap_slots(back_out, back_in, back_s, back_r, -1)
    everything += going_back
    sums["late"] = exchange_start("late", sums["late"])
    stay_pick = one_hot_lanes(column(jnp.where(to_row == 4.0, slot_row, -1.0)), ROWS)
    come_pick = one_hot_lanes(column(out_target), POOL)
    staying = dot(stay_pick, rounded)
    sums["early"] = spread_start("early", sums["early"])
    landed(going_back)
    refs["glat_v"][...] = (staying + dot(come_pick, back_in[...])).astype(BF16)
    put_result("glat_v", "glat_o")
    sums["late"] = spread_start("late", sums["late"])
    landed(sums["early"])
    put_result("final_early", "early_o")
    landed(sums["late"])
    put_result("final_late", "late_o")
    for copy in stored:
        copy.wait()
    for copy in everything:
        copy.wait_send()


def unpack(state, grad_latent, early, late, state_o, glat_o, gein_o, gehid_o, gnin_o, gnout_o, gbia_o, ggai_o):
    state_o[...] = state[...]
    glat_o[...] = grad_latent[...]
    sums = dict(early=early, late=late)

    def matrix(group, index):
        return sums[group][index * D : index * D + D, :].astype(F32)

    for layer in range(LAYERS):
        group, node = EDGE_GROUPS[layer], NODE_TERMS[layer]
        for index in range(2):
            gein_o[layer, index] = matrix(group, index)
            gehid_o[layer, index] = matrix(group, index + 2)
            gnin_o[layer, index] = matrix("early", node + index)
        gnout_o[layer] = matrix("early", node + 2)
    vectors = late[LATE_VECTORS : LATE_VECTORS + 16, :].astype(F32)
    for layer in range(LAYERS):
        first = 7 * (LAYERS - 1 - layer)
        gbia_o[:, layer] = vectors[first : first + 5]
        ggai_o[layer] = vectors[first + 5 : first + 7]


def shards(
    latent, move_to, move_slot, arrive_from, arrive_slot, neighbours, valid_count, face_send, corner_send,
    edge_in, edge_hid, node_in, node_out, biases, gains, grad_out,
):
    nx, ny = lax.axis_size("bx"), lax.axis_size("by")
    vmem = pl.BlockSpec(memory_space=pltpu.VMEM)
    shape = jax.ShapeDtypeStruct
    saved = pltpu.VMEM((LAYERS, PAIRS, ROWS, 2 * D), BF16)
    node = pltpu.VMEM((LAYERS, ROWS, D), F32)
    node_bf = pltpu.VMEM((LAYERS, ROWS, D), BF16)
    wide = pltpu.VMEM((LAYERS, 2 * D, 2 * D), BF16)
    dma = pltpu.SemaphoreType.DMA
    scratch = dict(
        outgoing=pltpu.VMEM((SLOTS, D), BF16),
        arrived=pltpu.VMEM((POOL, D), BF16),
        halo_out=pltpu.VMEM((LAYERS, HALO, D), BF16),
        halo_in=pltpu.VMEM((LAYERS, HALO, D), BF16),
        ret_out=pltpu.VMEM((LAYERS, HALO, D), BF16),
        ret_in=pltpu.VMEM((LAYERS, HALO, D), BF16),
        back_out=pltpu.VMEM((SLOTS, D), BF16),
        back_in=pltpu.VMEM((POOL, D), BF16),
        pick_send=pltpu.VMEM((HALO, ROWS), BF16),
        pick_back=pltpu.VMEM((ROWS, HALO), BF16),
        hits=pltpu.VMEM((K, ROWS, ROWS), BF16),
        hits_t=pltpu.VMEM((K, PLACES, ROWS), BF16),
        upper=pltpu.VMEM((K, ROWS, D), F32),
        count_col=pltpu.VMEM((ROWS, D), F32),
        state=node_bf,
        recv_term=pltpu.VMEM((ROWS, D), F32),
        own_tab=pltpu.VMEM((HALF, 2 * D), BF16),
        halo_tab=pltpu.VMEM((HALF, 2 * D), BF16),
        before=pltpu.VMEM((K, ROWS, D), F32),
        w_mid=wide,
        w_out=wide,
        w_mid_t=wide,
        w_out_t=wide,
        ones=pltpu.VMEM((2 * D, 2 * D), BF16),
        h1s=saved,
        h2s=saved,
        d1s=saved,
        d2s=saved,
        xhs=saved,
        rss=saved,
        acc=pltpu.VMEM((ROWS, D), F32),
        agg=node_bf,
        nhs=node_bf,
        d3s=node,
        xh2s=node,
        rs2s=node,
        dxc=pltpu.VMEM((ROWS, D), F32),
        g_recv=pltpu.VMEM((ROWS, D), F32),
        agg_raw=node,
        dsend=pltpu.VMEM((PLACES, 2 * D), F32),
        dw_out=pltpu.VMEM((D, D), F32),
        dw_mid=pltpu.VMEM((D, D), F32),
        db_out=pltpu.VMEM((8, 2 * D), F32),
        db_mid=pltpu.VMEM((8, 2 * D), F32),
        mig_s=dma((CODES,)),
        mig_r=dma((CODES,)),
        halo_s=dma((LAYERS, 8)),
        halo_r=dma((LAYERS, 8)),
        ret_s=dma((LAYERS, 8)),
        ret_r=dma((LAYERS, 8)),
        back_s=dma((CODES,)),
        back_r=dma((CODES,)),
        load_s=dma((16,)),
        store_s=dma((4,)),
        state_v=pltpu.VMEM((ROWS, D), BF16),
        glat_v=pltpu.VMEM((ROWS, D), BF16),
    )
    for group, total in (("early", EARLY_ROWS), ("late", LATE_ROWS)):
        chunk = total // ny
        scratch["terms_" + group] = pltpu.VMEM((total, D), BF16)
        scratch["rs_in_" + group] = pltpu.VMEM((ny - 1, chunk, D), BF16)
        scratch["ar_buf_" + group] = pltpu.VMEM((nx, chunk, D), BF16)
        scratch["final_" + group] = pltpu.VMEM((ny, chunk, D), BF16)
        for stage, partners in (("rs", ny), ("ar", nx), ("ag", ny)):
            scratch[f"{stage}_s_{group}"] = dma((partners - 1,))
            scratch[f"{stage}_r_{group}"] = dma((partners - 1,))

    def row(values):
        return values.reshape(1, ROWS)

    arguments = (
        latent, row(move_to), row(move_slot), row(arrive_from), row(arrive_slot),
        neighbours.T, row(valid_count), face_send.reshape(4, -1), corner_send.reshape(4, -1),
        edge_in, edge_hid, node_in, node_out, biases.transpose(1, 0, 2), gains, grad_out,
    )
    for name, value in zip(ARGUMENTS, arguments):
        scratch[name] = pltpu.VMEM(value.shape, value.dtype)
    names = ["arg_" + name for name in ARGUMENTS] + list(RESULTS) + list(scratch)
    state, grad_latent, early, late = pl.pallas_call(
        functools.partial(kernel, nx, ny, names),
        out_shape=(
            shape((ROWS, D), BF16),
            shape((ROWS, D), BF16),
            shape((ny, EARLY_ROWS // ny, D), BF16),
            shape((ny, LATE_ROWS // ny, D), BF16),
        ),
        in_specs=[pl.BlockSpec(memory_space=pl.ANY)] * len(ARGUMENTS),
        out_specs=(pl.BlockSpec(memory_space=pl.ANY),) * len(RESULTS),
        scratch_shapes=list(scratch.values()),
        compiler_params=pltpu.CompilerParams(
            collective_id=0, has_side_effects=True, vmem_limit_bytes=62 * 1024 * 1024
        ),
        name="evolve",
    )(*arguments)
    outputs = pl.pallas_call(
        unpack,
        out_shape=(
            shape((ROWS, D), BF16),
            shape((ROWS, D), BF16),
            shape((LAYERS, 2, D, D), F32),
            shape((LAYERS, 2, D, D), F32),
            shape((LAYERS, 2, D, D), F32),
            shape((LAYERS, D, D), F32),
            shape((5, LAYERS, D), F32),
            shape((LAYERS, 2, D), F32),
        ),
        in_specs=[vmem] * 4,
        out_specs=(vmem,) * 8,
        name="unpack",
    )(state, grad_latent, early.reshape(EARLY_ROWS, D), late.reshape(LATE_ROWS, D))
    return *outputs[:6], outputs[6].transpose(1, 0, 2), outputs[7]


def solution(mesh):
    both = ("bx", "by")
    rows, wide, grid = P(both), P(both, None), P("bx", "by", None, None)
    return jax.shard_map(
        shards,
        mesh=mesh,
        in_specs=(wide, rows, rows, rows, rows, wide, rows, grid, grid, P(), P(), P(), P(), P(), P(), wide),
        out_specs=(wide, wide, P(), P(), P(), P(), P(), P()),
        check_vma=False,
    )
```

```python
import functools

import jax
import jax.numpy as jnp
from jax import lax
from jax.experimental import pallas as pl
from jax.experimental.pallas import tpu as pltpu
from jax.sharding import PartitionSpec as P

LAYERS = 2
CAP = 32
D = 128
K = 16
PAIRS = K // 2
ROWS = 512
HALF = 256
HALO_HALF = 160
PLACES = HALF + HALO_HALF
HALO = 320
CODES = 9
SLOTS = CODES * CAP
POOL = 384
EARLY_ROWS = 1280
LATE_ROWS = 768
LATE_VECTORS = 512
BLOCK = 512
FORWARD_PAIRS = 4
BACKWARD_PAIRS = 4
F32 = jnp.float32
BF16 = jnp.bfloat16
MESH = pl.DeviceIdType.MESH
TRAVEL = tuple((code // 3 - 1, code % 3 - 1) for code in range(CODES))
HALO_BLOCKS = (
    (1, 0, 0, 64),
    (-1, 0, 64, 64),
    (0, 1, 128, 64),
    (0, -1, 192, 64),
    (1, 1, 256, 16),
    (1, -1, 272, 16),
    (-1, 1, 288, 16),
    (-1, -1, 304, 16),
)

ARGUMENTS = (
    "lat", "move_to", "move_slot", "arrive_from", "arrive_slot", "nbr", "count", "face", "corner",
    "e_in", "e_hid", "n_in", "n_out", "bia", "gai", "gout",
)
RESULTS = ("state_o", "glat_o", "early_o", "late_o")
SCRATCH = (
    "outgoing", "arrived", "halo_out", "halo_in", "ret_out", "ret_in", "back_out", "back_in",
    "pick_send", "pick_back", "hits", "hits_t", "upper", "count_col", "state", "recv_term",
    "own_tab", "halo_tab", "before", "w_mid", "w_out", "w_mid_t", "w_out_t", "ones", "h1s", "h2s", "d1s", "d2s", "xhs",
    "rss", "acc", "agg", "nhs", "d3s", "xh2s", "rs2s", "dxc", "g_recv", "agg_raw", "dsend",
    "dw_out", "dw_mid", "db_out", "db_mid", "mig_s", "mig_r", "halo_s", "halo_r", "ret_s", "ret_r",
    "back_s", "back_r",
)
EDGE_GROUPS = ("late", "early")
NODE_TERMS = (7, 4)


def dot(a, b):
    return jnp.dot(a, b, preferred_element_type=F32)


def dot_nt(a, b):
    return lax.dot_general(a, b, (((1,), (1,)), ((), ())), preferred_element_type=F32)


def dot_tn(a, b):
    return lax.dot_general(a, b, (((0,), (0,)), ((), ())), preferred_element_type=F32)


def column(row):
    return jnp.transpose(jnp.broadcast_to(row, (D, row.shape[1])))


def one_hot_lanes(filled, width):
    lane = lax.broadcasted_iota(jnp.int32, filled.shape, 1).astype(F32)
    pieces = [
        jnp.where(filled == lane + float(start), 1.0, 0.0).astype(BF16) for start in range(0, width, D)
    ]
    return jnp.concatenate(pieces, axis=1)


def one_hot_rows(row, height):
    index = lax.broadcasted_iota(jnp.int32, (height, row.shape[1]), 0).astype(F32)
    return jnp.where(index == row, 1.0, 0.0).astype(BF16)


def twice(values):
    return jnp.concatenate([values, values], axis=1)


def partial_sums(values):
    return jnp.sum(values.reshape(values.shape[0] // 8, 8, values.shape[1]), axis=0)


def staggered(chain, pairs):
    def body(group, carry):
        waiting = [
            chain(group * pairs + pair, first) for pair in range(pairs) for first in range(0, ROWS, BLOCK)
        ]
        running = []
        while waiting or running:
            if waiting:
                running.append(waiting.pop(0))
            running = [one for one in running if next(one, True) is None]
        return carry

    lax.fori_loop(0, PAIRS // pairs, body, 0)


def far_first(copies):
    middle = (len(copies) - 1) / 2
    return [copies[index] for index in sorted(range(len(copies)), key=lambda index: abs(index - middle))]


def layer_norm_parts(values):
    centred = values - jnp.mean(values, axis=1, keepdims=True)
    scale = lax.rsqrt(jnp.mean(centred * centred, axis=1, keepdims=True) + 1e-05)
    return centred * scale, scale


def half_silu(half):
    half = half.astype(BF16)
    wave = jnp.tanh(half)
    gate = 1.0 + wave
    value = half * gate
    return value, gate + value * (1.0 - wave)


def kernel(
    nx, ny, names, *refs
):
    refs = dict(zip(names, refs))
    arguments = [(refs["arg_" + name], refs[name]) for name in ARGUMENTS]
    (
        lat, move_to, move_slot, arrive_from, arrive_slot, nbr, count, face, corner,
        e_in, e_hid, n_in, n_out, bia, gai, gout,
    ) = (local for _, local in arguments)
    (
        outgoing, arrived, halo_out, halo_in, ret_out, ret_in, back_out, back_in,
        pick_send, pick_back, hits, hits_t, upper, count_col,
        state, recv_term, own_tab, halo_tab, before, w_mid, w_out, w_mid_t, w_out_t, ones,
        h1s, h2s, d1s, d2s, xhs, rss, acc, agg, nhs, d3s, xh2s, rs2s,
        dxc, g_recv, agg_raw, dsend, dw_out, dw_mid, db_out, db_mid,
        mig_s, mig_r, halo_s, halo_r, ret_s, ret_r, back_s, back_r,
    ) = (refs[name] for name in SCRATCH)
    a = lax.axis_index("bx")
    b = lax.axis_index("by")

    def at(move_x, move_y):
        return (lax.rem(a + (move_x + nx), nx), lax.rem(b + (move_y + ny), ny))

    def remote(src, dst, send, recv, target):
        return pltpu.make_async_remote_copy(
            src_ref=src, dst_ref=dst, send_sem=send, recv_sem=recv, device_id=target, device_id_type=MESH
        )

    barrier = pltpu.get_barrier_semaphore()
    partners = [(0, step) for step in range(1, ny)] + [(step, 0) for step in range(1, nx)]
    partners += [(1, 1), (1, -1), (-1, 1), (-1, -1)]
    for move_x, move_y in partners:
        pl.semaphore_signal(barrier, inc=1, device_id=at(move_x, move_y), device_id_type=MESH)

    loads = [
        pltpu.make_async_copy(there, here, refs["load_s"].at[index])
        for index, (there, here) in enumerate(arguments)
    ]
    for load in loads:
        load.start()
    for load in loads[:9]:
        load.wait()

    def as_row(ref):
        return ref[...].astype(F32)

    to_row, slot_row = as_row(move_to), as_row(move_slot)
    from_row, aslot_row = as_row(arrive_from), as_row(arrive_slot)
    out_target = jnp.where(to_row == 4.0, -1.0, to_row * CAP + slot_row)
    outgoing[...] = dot(one_hot_rows(out_target, SLOTS), lat[...]).astype(BF16)
    arrived[CAP * 4 : CAP * 5, :] = jnp.zeros((CAP, D), BF16)
    arrived[SLOTS:, :] = jnp.zeros((POOL - SLOTS, D), BF16)
    back_in[CAP * 4 : CAP * 5, :] = jnp.zeros((CAP, D), BF16)
    back_in[SLOTS:, :] = jnp.zeros((POOL - SLOTS, D), BF16)
    pl.semaphore_wait(barrier, len(partners))

    def swap_slots(source, target, send, recv, sign):
        copies = {}
        for code, (move_x, move_y) in enumerate(TRAVEL):
            if code == 4:
                continue
            rows = pl.ds(code * CAP, CAP)
            copies[code] = remote(
                source.at[rows], target.at[rows], send.at[code], recv.at[code],
                at(sign * move_x, sign * move_y),
            )
        for code in (0, 2, 6, 8, 1, 7, 3, 5):
            copies[code].start()
        return list(copies.values())

    def swap_halo(source, target, send, recv, sign):
        copies = []
        for index, (move_x, move_y, first, size) in enumerate(HALO_BLOCKS):
            rows = pl.ds(first, size)
            copies.append(
                remote(
                    source.at[rows], target.at[rows], send.at[index], recv.at[index],
                    at(sign * move_x, sign * move_y),
                )
            )
        for copy in copies[4:] + copies[:4]:
            copy.start()
        return copies

    def landed(copies):
        for copy in copies:
            copy.wait_recv()

    everything = []
    stored = []

    def put_result(local, result):
        copy = pltpu.make_async_copy(refs[local], refs[result], refs["store_s"].at[len(stored)])
        copy.start()
        stored.append(copy)

    migration = swap_slots(outgoing, arrived, mig_s, mig_r, 1)
    everything += migration

    stay_pick = one_hot_lanes(column(jnp.where(from_row == 4.0, aslot_row, -1.0)), ROWS)
    come_pick = one_hot_lanes(column(jnp.where(from_row == 4.0, -1.0, from_row * CAP + aslot_row)), POOL)
    staying = dot(stay_pick, lat[...])
    for index in range(4):
        filled = column(face[index : index + 1, :].astype(F32))
        pick_send[index * 64 : index * 64 + 64, :] = one_hot_lanes(filled, ROWS)
    for index in range(4):
        filled = column(corner[index : index + 1, :].astype(F32))
        pick_send[256 + index * 16 : 272 + index * 16, :] = one_hot_lanes(filled, ROWS)
    count_col[...] = column(as_row(count))

    def placed(row):
        halo = row - float(ROWS)
        own_high = row >= float(HALF)
        halo_high = halo >= float(HALO_HALF)
        own_place = jnp.where(own_high, row - float(HALF), row)
        halo_place = jnp.where(halo_high, halo - float(HALO_HALF), halo) + float(HALF)
        own = row < float(ROWS)
        high = jnp.where(own, jnp.where(own_high, 1.0, 0.0), jnp.where(halo_high, 1.0, 0.0))
        return jnp.where(own, own_place, halo_place), high

    def build_hits(k, carry):
        place, high = placed(nbr[pl.ds(k, 1), :].astype(F32))
        hits[k] = one_hot_lanes(column(place), ROWS)
        upper[k] = column(high)
        return carry

    lax.fori_loop(0, K, build_hits, 0)

    def build_hits_t(k, carry):
        hits_t[k] = one_hot_rows(placed(nbr[pl.ds(k, 1), :].astype(F32))[0], PLACES)
        return carry

    for load in loads[9:]:
        load.wait()

    diag = (lax.broadcasted_iota(jnp.int32, (2 * D, 2 * D), 0) // D) == (
        lax.broadcasted_iota(jnp.int32, (2 * D, 2 * D), 1) // D
    )
    ones[...] = jnp.where(diag, 1.0 / D, 0.0).astype(BF16)

    def doubled(weight):
        both = jnp.concatenate([twice(weight), twice(weight)], axis=0)
        return jnp.where(diag, both, 0.0).astype(BF16)

    for layer in range(LAYERS):
        mid = e_hid[layer, 0].astype(F32) * 0.5
        out = e_hid[layer, 1].astype(F32)
        w_mid[layer] = doubled(mid)
        w_out[layer] = doubled(out - jnp.mean(out, axis=1, keepdims=True))
    halo_tab[HALO_HALF:, :] = jnp.zeros((HALF - HALO_HALF, 2 * D), BF16)

    def bias(layer, index):
        return bia[index, layer : layer + 1, :]

    def gain(layer, index):
        return gai[layer, index : index + 1, :]

    def later_uses():
        lax.fori_loop(0, K, build_hits_t, 0)
        pick_back[...] = jnp.transpose(pick_send[...].astype(F32)).astype(BF16)

    def later_weights():
        for layer in range(LAYERS):
            w_mid_t[layer] = doubled(jnp.transpose(e_hid[layer, 0].astype(F32)) * 0.5)
            w_out_t[layer] = doubled(jnp.transpose(e_hid[layer, 1].astype(F32)) * 0.5)

    landed(migration)
    state[0] = (staying + dot(come_pick, arrived[...])).astype(BF16)

    def forward(layer, meanwhile):
        halo_out[layer] = dot(pick_send[...], state[layer]).astype(BF16)
        halo = swap_halo(halo_out.at[layer], halo_in.at[layer], halo_s.at[layer], halo_r.at[layer], 1)
        everything.extend(halo)
        own = state[layer]
        recv_term[...] = (dot(own, e_in[layer, 0]) + bias(layer, 0)) * 0.5
        w_send = (e_in[layer, 1].astype(F32) * 0.5).astype(BF16)
        own_send = dot(own, w_send).astype(BF16)
        own_tab[:, :D] = own_send[:HALF]
        own_tab[:, D:] = own_send[HALF:]
        acc[...] = jnp.zeros((ROWS, D), F32)
        bias_mid = twice(bias(layer, 1)) * 0.5
        bias_out = bias(layer, 2)
        bias_out = twice(bias_out - jnp.mean(bias_out, axis=1, keepdims=True))
        meanwhile()

        def own_chain(j, first):
            rows = slice(first, first + BLOCK)
            slots = (j, j + PAIRS)
            both = [dot(hits[k, rows, :HALF], own_tab[...]) for k in slots]
            yield
            for k, pick in zip(slots, both):
                before[k, rows] = recv_term[rows] + jnp.where(upper[k, rows] > 0.5, pick[:, D:], pick[:, :D])

        staggered(own_chain, 4)
        landed(halo)
        halo_send = dot(halo_in[layer], w_send).astype(BF16)
        halo_tab[:HALO_HALF, :D] = halo_send[:HALO_HALF]
        halo_tab[:HALO_HALF, D:] = halo_send[HALO_HALF:]

        def chain(j, first):
            rows = slice(first, first + BLOCK)
            both = [dot(hits[k, rows, HALF:], halo_tab[...]) for k in (j, j + PAIRS)]
            yield
            parts = [
                before[k, rows] + jnp.where(upper[k, rows] > 0.5, pick[:, D:], pick[:, :D])
                for k, pick in zip((j, j + PAIRS), both)
            ]
            value, slope = half_silu(jnp.concatenate(parts, axis=1))
            value = value.astype(BF16)
            h1s[layer, j, rows] = value
            d1s[layer, j, rows] = slope.astype(BF16)
            product = dot(value, w_mid[layer])
            yield
            value, slope = half_silu(product + bias_mid)
            value = value.astype(BF16)
            h2s[layer, j, rows] = value
            d2s[layer, j, rows] = slope.astype(BF16)
            product = dot(value, w_out[layer])
            yield
            centred = product + bias_out
            variance = dot((centred * centred).astype(BF16), ones[...])
            yield
            scale = lax.rsqrt(variance + 1e-05)
            live = count_col[rows]
            low_slot = jnp.float32(j) if isinstance(j, int) else j.astype(F32)
            mask = jnp.concatenate([live > low_slot, live > low_slot + PAIRS], axis=1)
            scale = jnp.where(mask, scale, 0.0)
            normed = centred * scale
            rss[layer, j, rows] = scale.astype(BF16)
            xhs[layer, j, rows] = normed.astype(BF16)
            acc[rows] += normed[:, :D] + normed[:, D:]

        staggered(chain, FORWARD_PAIRS)
        total = acc[...]
        agg_raw[layer] = total
        total = (total * gain(layer, 0)).astype(BF16)
        agg[layer] = total
        half = (dot(own, n_in[layer, 0]) + dot(total, n_in[layer, 1]) + bias(layer, 3)) * 0.5
        value, slope = half_silu(half)
        value = value.astype(BF16)
        nhs[layer] = value
        d3s[layer] = slope.astype(F32)
        normed, scale = layer_norm_parts(dot(value, n_out[layer]) + bias(layer, 4))
        xh2s[layer] = normed
        rs2s[layer] = jnp.broadcast_to(scale, (ROWS, D))
        return (own.astype(F32) + normed * gain(layer, 1)).astype(BF16)

    for layer in range(LAYERS):
        following = forward(layer, (later_uses, later_weights)[layer])
        if layer + 1 < LAYERS:
            state[layer + 1] = following
        else:
            refs["state_v"][...] = following
            put_result("state_v", "state_o")

    def put_term(group, index, values):
        refs["terms_" + group][index * D : index * D + D, :] = values.astype(BF16)

    def reduce_start(group):
        terms, arriving = refs["terms_" + group], refs["rs_in_" + group]
        chunk = arriving.shape[1]
        copies = []
        for step in range(1, ny):
            peer = lax.rem(b + step, ny)
            rows = pl.ds(pl.multiple_of(peer * chunk, chunk), chunk)
            sems = (refs["rs_s_" + group].at[step - 1], refs["rs_r_" + group].at[step - 1])
            copies.append(remote(terms.at[rows], arriving.at[step - 1], *sems, (a, peer)))
        for copy in far_first(copies):
            copy.start()
        everything.extend(copies)
        return copies

    def exchange_start(group, reducing):
        terms, arriving, summed = refs["terms_" + group], refs["rs_in_" + group], refs["ar_buf_" + group]
        chunk = arriving.shape[1]
        landed(reducing)
        total = terms[pl.ds(pl.multiple_of(b * chunk, chunk), chunk), :].astype(F32)
        for step in range(ny - 1):
            total = total + arriving[step].astype(F32)
        summed[a] = total.astype(BF16)
        out, come = [], []
        for step in range(1, nx):
            peer = lax.rem(a + step, nx)
            source = lax.rem(a + (nx - step), nx)
            sems = (refs["ar_s_" + group].at[step - 1], refs["ar_r_" + group].at[step - 1])
            out.append(remote(summed.at[a], summed.at[a], *sems, (peer, b)))
            come.append(remote(summed.at[source], summed.at[source], *sems, (peer, b)))
        for copy in far_first(out):
            copy.start()
        everything.extend(out)
        return come

    def spread_start(group, exchanging):
        summed, final = refs["ar_buf_" + group], refs["final_" + group]
        landed(exchanging)
        total = summed[0].astype(F32)
        for step in range(1, nx):
            total = total + summed[step].astype(F32)
        final[b] = total.astype(BF16)
        out, come = [], []
        for step in range(1, ny):
            peer = lax.rem(b + step, ny)
            source = lax.rem(b + (ny - step), ny)
            sems = (refs["ag_s_" + group].at[step - 1], refs["ag_r_" + group].at[step - 1])
            out.append(remote(final.at[b], final.at[b], *sems, (a, peer)))
            come.append(remote(final.at[source], final.at[source], *sems, (a, peer)))
        for copy in far_first(out):
            copy.start()
        everything.extend(out)
        return come

    vectors = []

    def backward(layer, cotangent, before_edges):
        own = state[layer]
        normed = xh2s[layer]
        lifted = cotangent * gain(layer, 1)
        grad_gain_node = jnp.sum(cotangent * normed, axis=0, keepdims=True)
        inner = jnp.mean(lifted * normed, axis=1, keepdims=True)
        grad = rs2s[layer] * (lifted - jnp.mean(lifted, axis=1, keepdims=True) - normed * inner)
        grad_b4 = jnp.sum(grad, axis=0, keepdims=True)
        grad = grad.astype(BF16)
        put_term("early", NODE_TERMS[layer] + 2, dot_tn(nhs[layer], grad))
        grad = dot_nt(grad, n_out[layer]) * (d3s[layer] * 0.5)
        grad_b3 = jnp.sum(grad, axis=0, keepdims=True)
        grad = grad.astype(BF16)
        put_term("early", NODE_TERMS[layer], dot_tn(own, grad))
        put_term("early", NODE_TERMS[layer] + 1, dot_tn(agg[layer], grad))
        own_grad = cotangent + dot_nt(grad, n_in[layer, 0])
        grad_agg = dot_nt(grad, n_in[layer, 1])
        grad_gain_edge = jnp.sum(grad_agg * agg_raw[layer], axis=0, keepdims=True)
        lifted = grad_agg * gain(layer, 0)
        dxc[...] = lifted - jnp.mean(lifted, axis=1, keepdims=True)
        g_recv[...] = jnp.zeros((ROWS, D), F32)
        dsend[...] = jnp.zeros((PLACES, 2 * D), F32)
        dw_out[...] = jnp.zeros((D, D), F32)
        dw_mid[...] = jnp.zeros((D, D), F32)
        db_out[...] = jnp.zeros((8, 2 * D), F32)
        db_mid[...] = jnp.zeros((8, 2 * D), F32)
        before_edges()

        later = layer == LAYERS - 1
        lowest = HALF if later else 0

        def add_hidden(total, hidden, grad):
            total[...] += dot_tn(hidden[:, :D], grad[:, :D]) + dot_tn(hidden[:, D:], grad[:, D:])

        def chain(j, first):
            rows = slice(first, first + BLOCK)
            lift = twice(dxc[rows])
            unit = xhs[layer, j, rows].astype(F32)
            shared = dot((lift * unit).astype(BF16), ones[...])
            yield
            grad = rss[layer, j, rows].astype(F32) * (lift - unit * shared)
            db_out[...] += partial_sums(grad)
            grad = grad.astype(BF16)
            product = dot(grad, w_out_t[layer])
            if later:
                hits[j, rows, HALF:] = grad
            else:
                add_hidden(dw_out, h2s[layer, j, rows], grad)
            yield
            grad = product * d2s[layer, j, rows].astype(F32)
            db_mid[...] += partial_sums(grad)
            grad = grad.astype(BF16)
            product = dot(grad, w_mid_t[layer])
            if later:
                hits[j + PAIRS, rows, HALF:] = grad
            else:
                add_hidden(dw_mid, h1s[layer, j, rows], grad)
            yield
            grad = product * d1s[layer, j, rows].astype(F32)
            g_recv[rows] += grad[:, :D] + grad[:, D:]
            scattered = None
            for part in range(2):
                k = j + part * PAIRS
                piece = grad[:, part * D : part * D + D]
                high = upper[k, rows] > 0.5
                split = jnp.concatenate([jnp.where(high, 0.0, piece), jnp.where(high, piece, 0.0)], axis=1)
                split = split.astype(BF16)
                if later:
                    hits[k, rows, :HALF] = split
                added = dot(hits_t[k, lowest:, rows], split)
                scattered = added if scattered is None else scattered + added
            dsend[lowest:] += scattered

        staggered(chain, BACKWARD_PAIRS)
        halo_grad = dsend[HALF:].astype(BF16)
        halo_grad = jnp.concatenate([halo_grad[:, :D], halo_grad[:, D:]], axis=0)

        def send_back():
            ret_out[layer] = dot_nt(halo_grad, e_in[layer, 1]).astype(BF16)
            copies = swap_halo(ret_out.at[layer], ret_in.at[layer], ret_s.at[layer], ret_r.at[layer], -1)
            everything.extend(copies)
            return copies

        if later:
            returning = send_back()

            def rest(j, first):
                rows = slice(first, first + BLOCK)
                dsend[:HALF] += sum(dot(hits_t[k, :HALF, rows], hits[k, rows, :HALF]) for k in (j, j + PAIRS))
                add_hidden(dw_out, h2s[layer, j, rows], hits[j, rows, HALF:])
                add_hidden(dw_mid, h1s[layer, j, rows], hits[j + PAIRS, rows, HALF:])
                yield

            staggered(rest, 2)
        send_own = dsend[:HALF].astype(BF16)
        send_own = jnp.concatenate([send_own[:, :D], send_own[:, D:]], axis=0)
        term = dot_tn(own, send_own) + dot_tn(halo_in[layer], halo_grad)
        group = EDGE_GROUPS[layer]
        put_term(group, 1, term)
        grad = g_recv[...]
        grad_b0 = jnp.sum(grad, axis=0, keepdims=True)
        grad = grad.astype(BF16)
        put_term(group, 0, dot_tn(own, grad))
        put_term(group, 2, dw_mid[...])
        put_term(group, 3, dw_out[...])
        total_mid = jnp.sum(db_mid[...], axis=0, keepdims=True)
        total_out = jnp.sum(db_out[...], axis=0, keepdims=True)
        vectors.extend([
            grad_b0,
            total_mid[:, :D] + total_mid[:, D:],
            total_out[:, :D] + total_out[:, D:],
            grad_b3,
            grad_b4,
            grad_gain_edge,
            grad_gain_node,
        ])
        if not later:
            late_start()
            returning = send_back()
        own_grad = own_grad + dot_nt(grad, e_in[layer, 0]) + dot_nt(send_own, e_in[layer, 1])
        if not later:
            prepare_end()
        landed(returning)
        own_grad = own_grad + dot(pick_back[...], ret_in[layer])
        return own_grad.astype(BF16)

    sums = {}

    def early_start():
        sums["early"] = reduce_start("early")

    def late_start():
        terms = refs["terms_late"]
        terms[LATE_VECTORS:, :] = jnp.zeros((LATE_ROWS - LATE_VECTORS, D), BF16)
        stacked = jnp.concatenate(vectors + [jnp.zeros((2, D), F32)], axis=0)
        terms[LATE_VECTORS : LATE_VECTORS + 16, :] = stacked.astype(BF16)
        sums["late"] = reduce_start("late")

    def prepare_end():
        sums["early"] = exchange_start("early", sums["early"])
        back_target = jnp.where(from_row == 4.0, -1.0, from_row * CAP + aslot_row)
        hits[0, :SLOTS, :] = one_hot_rows(back_target, SLOTS)
        hits[1] = one_hot_lanes(column(jnp.where(to_row == 4.0, slot_row, -1.0)), ROWS)
        hits[2, :, :POOL] = one_hot_lanes(column(out_target), POOL)
        sums["late"] = exchange_start("late", sums["late"])

    rounded = backward(1, gout[...].astype(F32), lambda: None)
    rounded = backward(0, rounded.astype(F32), early_start)

    back_out[...] = dot(hits[0, :SLOTS, :], rounded).astype(BF16)
    going_back = swap_slots(back_out, back_in, back_s, back_r, -1)
    everything += going_back
    staying = dot(hits[1], rounded)
    sums["early"] = spread_start("early", sums["early"])
    sums["late"] = spread_start("late", sums["late"])
    landed(going_back)
    refs["glat_v"][...] = (staying + dot(hits[2, :, :POOL], back_in[...])).astype(BF16)
    put_result("glat_v", "glat_o")
    landed(sums["early"])
    put_result("final_early", "early_o")
    landed(sums["late"])
    put_result("final_late", "late_o")
    for copy in stored:
        copy.wait()
    for copy in everything:
        copy.wait_send()


def unpack(state, grad_latent, early, late, state_o, glat_o, gein_o, gehid_o, gnin_o, gnout_o, gbia_o, ggai_o):
    state_o[...] = state[...]
    glat_o[...] = grad_latent[...]
    sums = dict(early=early, late=late)

    def matrix(group, index):
        return sums[group][index * D : index * D + D, :].astype(F32)

    for layer in range(LAYERS):
        group, node = EDGE_GROUPS[layer], NODE_TERMS[layer]
        for index in range(2):
            gein_o[layer, index] = matrix(group, index)
            gehid_o[layer, index] = matrix(group, index + 2)
            gnin_o[layer, index] = matrix("early", node + index)
        gnout_o[layer] = matrix("early", node + 2)
    vectors = late[LATE_VECTORS : LATE_VECTORS + 16, :].astype(F32)
    for layer in range(LAYERS):
        first = 7 * (LAYERS - 1 - layer)
        gbia_o[:, layer] = vectors[first : first + 5]
        ggai_o[layer] = vectors[first + 5 : first + 7]


def shards(
    latent, move_to, move_slot, arrive_from, arrive_slot, neighbours, valid_count, face_send, corner_send,
    edge_in, edge_hid, node_in, node_out, biases, gains, grad_out,
):
    nx, ny = lax.axis_size("bx"), lax.axis_size("by")
    vmem = pl.BlockSpec(memory_space=pltpu.VMEM)
    shape = jax.ShapeDtypeStruct
    saved = pltpu.VMEM((LAYERS, PAIRS, ROWS, 2 * D), BF16)
    node = pltpu.VMEM((LAYERS, ROWS, D), F32)
    node_bf = pltpu.VMEM((LAYERS, ROWS, D), BF16)
    wide = pltpu.VMEM((LAYERS, 2 * D, 2 * D), BF16)
    dma = pltpu.SemaphoreType.DMA
    scratch = dict(
        outgoing=pltpu.VMEM((SLOTS, D), BF16),
        arrived=pltpu.VMEM((POOL, D), BF16),
        halo_out=pltpu.VMEM((LAYERS, HALO, D), BF16),
        halo_in=pltpu.VMEM((LAYERS, HALO, D), BF16),
        ret_out=pltpu.VMEM((LAYERS, HALO, D), BF16),
        ret_in=pltpu.VMEM((LAYERS, HALO, D), BF16),
        back_out=pltpu.VMEM((SLOTS, D), BF16),
        back_in=pltpu.VMEM((POOL, D), BF16),
        pick_send=pltpu.VMEM((HALO, ROWS), BF16),
        pick_back=pltpu.VMEM((ROWS, HALO), BF16),
        hits=pltpu.VMEM((K, ROWS, ROWS), BF16),
        hits_t=pltpu.VMEM((K, PLACES, ROWS), BF16),
        upper=pltpu.VMEM((K, ROWS, D), F32),
        count_col=pltpu.VMEM((ROWS, D), F32),
        state=node_bf,
        recv_term=pltpu.VMEM((ROWS, D), F32),
        own_tab=pltpu.VMEM((HALF, 2 * D), BF16),
        halo_tab=pltpu.VMEM((HALF, 2 * D), BF16),
        before=pltpu.VMEM((K, ROWS, D), F32),
        w_mid=wide,
        w_out=wide,
        w_mid_t=wide,
        w_out_t=wide,
        ones=pltpu.VMEM((2 * D, 2 * D), BF16),
        h1s=saved,
        h2s=saved,
        d1s=saved,
        d2s=saved,
        xhs=saved,
        rss=saved,
        acc=pltpu.VMEM((ROWS, D), F32),
        agg=node_bf,
        nhs=node_bf,
        d3s=node,
        xh2s=node,
        rs2s=node,
        dxc=pltpu.VMEM((ROWS, D), F32),
        g_recv=pltpu.VMEM((ROWS, D), F32),
        agg_raw=node,
        dsend=pltpu.VMEM((PLACES, 2 * D), F32),
        dw_out=pltpu.VMEM((D, D), F32),
        dw_mid=pltpu.VMEM((D, D), F32),
        db_out=pltpu.VMEM((8, 2 * D), F32),
        db_mid=pltpu.VMEM((8, 2 * D), F32),
        mig_s=dma((CODES,)),
        mig_r=dma((CODES,)),
        halo_s=dma((LAYERS, 8)),
        halo_r=dma((LAYERS, 8)),
        ret_s=dma((LAYERS, 8)),
        ret_r=dma((LAYERS, 8)),
        back_s=dma((CODES,)),
        back_r=dma((CODES,)),
        load_s=dma((16,)),
        store_s=dma((4,)),
        state_v=pltpu.VMEM((ROWS, D), BF16),
        glat_v=pltpu.VMEM((ROWS, D), BF16),
    )
    for group, total in (("early", EARLY_ROWS), ("late", LATE_ROWS)):
        chunk = total // ny
        scratch["terms_" + group] = pltpu.VMEM((total, D), BF16)
        scratch["rs_in_" + group] = pltpu.VMEM((ny - 1, chunk, D), BF16)
        scratch["ar_buf_" + group] = pltpu.VMEM((nx, chunk, D), BF16)
        scratch["final_" + group] = pltpu.VMEM((ny, chunk, D), BF16)
        for stage, partners in (("rs", ny), ("ar", nx), ("ag", ny)):
            scratch[f"{stage}_s_{group}"] = dma((partners - 1,))
            scratch[f"{stage}_r_{group}"] = dma((partners - 1,))

    def row(values):
        return values.reshape(1, ROWS)

    arguments = (
        latent, row(move_to), row(move_slot), row(arrive_from), row(arrive_slot),
        neighbours.T, row(valid_count), face_send.reshape(4, -1), corner_send.reshape(4, -1),
        edge_in, edge_hid, node_in, node_out, biases.transpose(1, 0, 2), gains, grad_out,
    )
    for name, value in zip(ARGUMENTS, arguments):
        scratch[name] = pltpu.VMEM(value.shape, value.dtype)
    names = ["arg_" + name for name in ARGUMENTS] + list(RESULTS) + list(scratch)
    state, grad_latent, early, late = pl.pallas_call(
        functools.partial(kernel, nx, ny, names),
        out_shape=(
            shape((ROWS, D), BF16),
            shape((ROWS, D), BF16),
            shape((ny, EARLY_ROWS // ny, D), BF16),
            shape((ny, LATE_ROWS // ny, D), BF16),
        ),
        in_specs=[pl.BlockSpec(memory_space=pl.ANY)] * len(ARGUMENTS),
        out_specs=(pl.BlockSpec(memory_space=pl.ANY),) * len(RESULTS),
        scratch_shapes=list(scratch.values()),
        compiler_params=pltpu.CompilerParams(
            collective_id=0, has_side_effects=True, vmem_limit_bytes=62 * 1024 * 1024
        ),
        name="evolve",
    )(*arguments)
    outputs = pl.pallas_call(
        unpack,
        out_shape=(
            shape((ROWS, D), BF16),
            shape((ROWS, D), BF16),
            shape((LAYERS, 2, D, D), F32),
            shape((LAYERS, 2, D, D), F32),
            shape((LAYERS, 2, D, D), F32),
            shape((LAYERS, D, D), F32),
            shape((5, LAYERS, D), F32),
            shape((LAYERS, 2, D), F32),
        ),
        in_specs=[vmem] * 4,
        out_specs=(vmem,) * 8,
        name="unpack",
    )(state, grad_latent, early.reshape(EARLY_ROWS, D), late.reshape(LATE_ROWS, D))
    return *outputs[:6], outputs[6].transpose(1, 0, 2), outputs[7]


def solution(mesh):
    both = ("bx", "by")
    rows, wide, grid = P(both), P(both, None), P("bx", "by", None, None)
    return jax.shard_map(
        shards,
        mesh=mesh,
        in_specs=(wide, rows, rows, rows, rows, wide, rows, grid, grid, P(), P(), P(), P(), P(), P(), wide),
        out_specs=(wide, wide, P(), P(), P(), P(), P(), P()),
        check_vma=False,
    )
```

```python
import functools

import jax
import jax.numpy as jnp
from jax import lax
from jax.experimental import pallas as pl
from jax.experimental.pallas import tpu as pltpu
from jax.sharding import PartitionSpec as P

LAYERS = 2
CAP = 32
D = 128
K = 16
PAIRS = K // 2
ROWS = 512
HALF = 256
HALO_HALF = 160
PLACES = HALF + HALO_HALF
HALO = 320
CODES = 9
SLOTS = CODES * CAP
POOL = 384
EARLY_ROWS = 1280
LATE_ROWS = 768
LATE_VECTORS = 512
BLOCK = 512
FORWARD_PAIRS = 4
BACKWARD_PAIRS = 4
F32 = jnp.float32
BF16 = jnp.bfloat16
MESH = pl.DeviceIdType.MESH
TRAVEL = tuple((code // 3 - 1, code % 3 - 1) for code in range(CODES))
HALO_BLOCKS = (
    (1, 0, 0, 64),
    (-1, 0, 64, 64),
    (0, 1, 128, 64),
    (0, -1, 192, 64),
    (1, 1, 256, 16),
    (1, -1, 272, 16),
    (-1, 1, 288, 16),
    (-1, -1, 304, 16),
)

ARGUMENTS = (
    "lat", "move_to", "move_slot", "arrive_from", "arrive_slot", "nbr", "count", "face", "corner",
    "e_in", "e_hid", "n_in", "n_out", "bia", "gai", "gout",
)
RESULTS = ("state_o", "glat_o", "early_o", "late_o")
SCRATCH = (
    "outgoing", "arrived", "halo_out", "halo_in", "ret_out", "ret_in", "back_out", "back_in",
    "pick_send", "pick_back", "hits", "hits_t", "upper", "count_col", "state", "recv_term",
    "own_tab", "halo_tab", "before", "w_mid", "w_out", "w_mid_t", "w_out_t", "ones", "h1s", "h2s", "d1s", "d2s", "xhs",
    "rss", "acc", "agg", "nhs", "d3s", "xh2s", "rs2s", "dxc", "g_recv", "agg_raw", "dsend",
    "dw_out", "dw_mid", "db_out", "db_mid", "mig_s", "mig_r", "halo_s", "halo_r", "ret_s", "ret_r",
    "back_s", "back_r",
)
EDGE_GROUPS = ("late", "early")
NODE_TERMS = (7, 4)


def dot(a, b):
    return jnp.dot(a, b, preferred_element_type=F32)


def dot_nt(a, b):
    return lax.dot_general(a, b, (((1,), (1,)), ((), ())), preferred_element_type=F32)


def dot_tn(a, b):
    return lax.dot_general(a, b, (((0,), (0,)), ((), ())), preferred_element_type=F32)


def column(row):
    return jnp.transpose(jnp.broadcast_to(row, (D, row.shape[1])))


def one_hot_lanes(filled, width):
    lane = lax.broadcasted_iota(jnp.int32, filled.shape, 1).astype(F32)
    pieces = [
        jnp.where(filled == lane + float(start), 1.0, 0.0).astype(BF16) for start in range(0, width, D)
    ]
    return jnp.concatenate(pieces, axis=1)


def one_hot_rows(row, height):
    index = lax.broadcasted_iota(jnp.int32, (height, row.shape[1]), 0).astype(F32)
    return jnp.where(index == row, 1.0, 0.0).astype(BF16)


def twice(values):
    return jnp.concatenate([values, values], axis=1)


def partial_sums(values):
    return jnp.sum(values.reshape(values.shape[0] // 8, 8, values.shape[1]), axis=0)


def staggered(chain, pairs):
    def body(group, carry):
        waiting = [
            chain(group * pairs + pair, first) for pair in range(pairs) for first in range(0, ROWS, BLOCK)
        ]
        running = []
        while waiting or running:
            if waiting:
                running.append(waiting.pop(0))
            running = [one for one in running if next(one, True) is None]
        return carry

    lax.fori_loop(0, PAIRS // pairs, body, 0)


def layer_norm_parts(values):
    centred = values - jnp.mean(values, axis=1, keepdims=True)
    scale = lax.rsqrt(jnp.mean(centred * centred, axis=1, keepdims=True) + 1e-05)
    return centred * scale, scale


def half_silu(half):
    half = half.astype(BF16)
    wave = jnp.tanh(half)
    gate = 1.0 + wave
    value = half * gate
    return value, gate + value * (1.0 - wave)


def kernel(
    nx, ny, names, *refs
):
    refs = dict(zip(names, refs))
    arguments = [(refs["arg_" + name], refs[name]) for name in ARGUMENTS]
    (
        lat, move_to, move_slot, arrive_from, arrive_slot, nbr, count, face, corner,
        e_in, e_hid, n_in, n_out, bia, gai, gout,
    ) = (local for _, local in arguments)
    (
        outgoing, arrived, halo_out, halo_in, ret_out, ret_in, back_out, back_in,
        pick_send, pick_back, hits, hits_t, upper, count_col,
        state, recv_term, own_tab, halo_tab, before, w_mid, w_out, w_mid_t, w_out_t, ones,
        h1s, h2s, d1s, d2s, xhs, rss, acc, agg, nhs, d3s, xh2s, rs2s,
        dxc, g_recv, agg_raw, dsend, dw_out, dw_mid, db_out, db_mid,
        mig_s, mig_r, halo_s, halo_r, ret_s, ret_r, back_s, back_r,
    ) = (refs[name] for name in SCRATCH)
    a = lax.axis_index("bx")
    b = lax.axis_index("by")

    def at(move_x, move_y):
        return (lax.rem(a + (move_x + nx), nx), lax.rem(b + (move_y + ny), ny))

    def remote(src, dst, send, recv, target):
        return pltpu.make_async_remote_copy(
            src_ref=src, dst_ref=dst, send_sem=send, recv_sem=recv, device_id=target, device_id_type=MESH
        )

    barrier = pltpu.get_barrier_semaphore()
    partners = [(0, step) for step in range(1, ny)] + [(step, 0) for step in range(1, nx)]
    partners += [(1, 1), (1, -1), (-1, 1), (-1, -1)]
    for move_x, move_y in partners:
        pl.semaphore_signal(barrier, inc=1, device_id=at(move_x, move_y), device_id_type=MESH)

    loads = [
        pltpu.make_async_copy(there, here, refs["load_s"].at[index])
        for index, (there, here) in enumerate(arguments)
    ]
    for load in loads:
        load.start()
    for load in loads[:9]:
        load.wait()

    def as_row(ref):
        return ref[...].astype(F32)

    to_row, slot_row = as_row(move_to), as_row(move_slot)
    from_row, aslot_row = as_row(arrive_from), as_row(arrive_slot)
    out_target = jnp.where(to_row == 4.0, -1.0, to_row * CAP + slot_row)
    outgoing[...] = dot(one_hot_rows(out_target, SLOTS), lat[...]).astype(BF16)
    arrived[CAP * 4 : CAP * 5, :] = jnp.zeros((CAP, D), BF16)
    arrived[SLOTS:, :] = jnp.zeros((POOL - SLOTS, D), BF16)
    back_in[CAP * 4 : CAP * 5, :] = jnp.zeros((CAP, D), BF16)
    back_in[SLOTS:, :] = jnp.zeros((POOL - SLOTS, D), BF16)
    pl.semaphore_wait(barrier, len(partners))

    def swap_slots(source, target, send, recv, sign):
        copies = {}
        for code, (move_x, move_y) in enumerate(TRAVEL):
            if code == 4:
                continue
            rows = pl.ds(code * CAP, CAP)
            copies[code] = remote(
                source.at[rows], target.at[rows], send.at[code], recv.at[code],
                at(sign * move_x, sign * move_y),
            )
        for code in (0, 1, 2, 3, 5, 6, 7, 8):
            copies[code].start()
        return list(copies.values())

    def swap_halo(source, target, send, recv, sign):
        copies = []
        for index, (move_x, move_y, first, size) in enumerate(HALO_BLOCKS):
            rows = pl.ds(first, size)
            copies.append(
                remote(
                    source.at[rows], target.at[rows], send.at[index], recv.at[index],
                    at(sign * move_x, sign * move_y),
                )
            )
        for copy in copies:
            copy.start()
        return copies

    def landed(copies):
        for copy in copies:
            copy.wait_recv()

    everything = []
    stored = []

    def put_result(local, result):
        copy = pltpu.make_async_copy(refs[local], refs[result], refs["store_s"].at[len(stored)])
        copy.start()
        stored.append(copy)

    migration = swap_slots(outgoing, arrived, mig_s, mig_r, 1)
    everything += migration

    stay_pick = one_hot_lanes(column(jnp.where(from_row == 4.0, aslot_row, -1.0)), ROWS)
    come_pick = one_hot_lanes(column(jnp.where(from_row == 4.0, -1.0, from_row * CAP + aslot_row)), POOL)
    staying = dot(stay_pick, lat[...])
    for index in range(4):
        filled = column(face[index : index + 1, :].astype(F32))
        pick_send[index * 64 : index * 64 + 64, :] = one_hot_lanes(filled, ROWS)
    for index in range(4):
        filled = column(corner[index : index + 1, :].astype(F32))
        pick_send[256 + index * 16 : 272 + index * 16, :] = one_hot_lanes(filled, ROWS)
    count_col[...] = column(as_row(count))

    def placed(row):
        halo = row - float(ROWS)
        own_high = row >= float(HALF)
        halo_high = halo >= float(HALO_HALF)
        own_place = jnp.where(own_high, row - float(HALF), row)
        halo_place = jnp.where(halo_high, halo - float(HALO_HALF), halo) + float(HALF)
        own = row < float(ROWS)
        high = jnp.where(own, jnp.where(own_high, 1.0, 0.0), jnp.where(halo_high, 1.0, 0.0))
        return jnp.where(own, own_place, halo_place), high

    def build_hits(k, carry):
        place, high = placed(nbr[pl.ds(k, 1), :].astype(F32))
        hits[k] = one_hot_lanes(column(place), ROWS)
        upper[k] = column(high)
        return carry

    lax.fori_loop(0, K, build_hits, 0)

    def build_hits_t(k, carry):
        hits_t[k] = one_hot_rows(placed(nbr[pl.ds(k, 1), :].astype(F32))[0], PLACES)
        return carry

    for load in loads[9:]:
        load.wait()

    diag = (lax.broadcasted_iota(jnp.int32, (2 * D, 2 * D), 0) // D) == (
        lax.broadcasted_iota(jnp.int32, (2 * D, 2 * D), 1) // D
    )
    ones[...] = jnp.where(diag, 1.0 / D, 0.0).astype(BF16)

    def doubled(weight):
        both = jnp.concatenate([twice(weight), twice(weight)], axis=0)
        return jnp.where(diag, both, 0.0).astype(BF16)

    for layer in range(LAYERS):
        mid = e_hid[layer, 0].astype(F32) * 0.5
        out = e_hid[layer, 1].astype(F32)
        w_mid[layer] = doubled(mid)
        w_out[layer] = doubled(out - jnp.mean(out, axis=1, keepdims=True))
    halo_tab[HALO_HALF:, :] = jnp.zeros((HALF - HALO_HALF, 2 * D), BF16)

    def bias(layer, index):
        return bia[index, layer : layer + 1, :]

    def gain(layer, index):
        return gai[layer, index : index + 1, :]

    def later_uses():
        lax.fori_loop(0, K, build_hits_t, 0)
        pick_back[...] = jnp.transpose(pick_send[...].astype(F32)).astype(BF16)

    def later_weights():
        for layer in range(LAYERS):
            w_mid_t[layer] = doubled(jnp.transpose(e_hid[layer, 0].astype(F32)) * 0.5)
            w_out_t[layer] = doubled(jnp.transpose(e_hid[layer, 1].astype(F32)) * 0.5)

    landed(migration)
    state[0] = (staying + dot(come_pick, arrived[...])).astype(BF16)

    def forward(layer, meanwhile):
        halo_out[layer] = dot(pick_send[...], state[layer]).astype(BF16)
        halo = swap_halo(halo_out.at[layer], halo_in.at[layer], halo_s.at[layer], halo_r.at[layer], 1)
        everything.extend(halo)
        own = state[layer]
        recv_term[...] = (dot(own, e_in[layer, 0]) + bias(layer, 0)) * 0.5
        w_send = (e_in[layer, 1].astype(F32) * 0.5).astype(BF16)
        own_send = dot(own, w_send).astype(BF16)
        own_tab[:, :D] = own_send[:HALF]
        own_tab[:, D:] = own_send[HALF:]
        acc[...] = jnp.zeros((ROWS, D), F32)
        bias_mid = twice(bias(layer, 1)) * 0.5
        bias_out = bias(layer, 2)
        bias_out = twice(bias_out - jnp.mean(bias_out, axis=1, keepdims=True))
        meanwhile()

        def own_chain(j, first):
            rows = slice(first, first + BLOCK)
            slots = (j, j + PAIRS)
            both = [dot(hits[k, rows, :HALF], own_tab[...]) for k in slots]
            yield
            for k, pick in zip(slots, both):
                before[k, rows] = recv_term[rows] + jnp.where(upper[k, rows] > 0.5, pick[:, D:], pick[:, :D])

        staggered(own_chain, 4)
        landed(halo)
        halo_send = dot(halo_in[layer], w_send).astype(BF16)
        halo_tab[:HALO_HALF, :D] = halo_send[:HALO_HALF]
        halo_tab[:HALO_HALF, D:] = halo_send[HALO_HALF:]

        def chain(j, first):
            rows = slice(first, first + BLOCK)
            both = [dot(hits[k, rows, HALF:], halo_tab[...]) for k in (j, j + PAIRS)]
            yield
            parts = [
                before[k, rows] + jnp.where(upper[k, rows] > 0.5, pick[:, D:], pick[:, :D])
                for k, pick in zip((j, j + PAIRS), both)
            ]
            value, slope = half_silu(jnp.concatenate(parts, axis=1))
            value = value.astype(BF16)
            h1s[layer, j, rows] = value
            d1s[layer, j, rows] = slope.astype(BF16)
            product = dot(value, w_mid[layer])
            yield
            value, slope = half_silu(product + bias_mid)
            value = value.astype(BF16)
            h2s[layer, j, rows] = value
            d2s[layer, j, rows] = slope.astype(BF16)
            product = dot(value, w_out[layer])
            yield
            centred = product + bias_out
            variance = dot((centred * centred).astype(BF16), ones[...])
            yield
            scale = lax.rsqrt(variance + 1e-05)
            live = count_col[rows]
            low_slot = jnp.float32(j) if isinstance(j, int) else j.astype(F32)
            mask = jnp.concatenate([live > low_slot, live > low_slot + PAIRS], axis=1)
            scale = jnp.where(mask, scale, 0.0)
            normed = centred * scale
            rss[layer, j, rows] = scale.astype(BF16)
            xhs[layer, j, rows] = normed.astype(BF16)
            acc[rows] += normed[:, :D] + normed[:, D:]

        staggered(chain, FORWARD_PAIRS)
        total = acc[...]
        agg_raw[layer] = total
        total = (total * gain(layer, 0)).astype(BF16)
        agg[layer] = total
        half = (dot(own, n_in[layer, 0]) + dot(total, n_in[layer, 1]) + bias(layer, 3)) * 0.5
        value, slope = half_silu(half)
        value = value.astype(BF16)
        nhs[layer] = value
        d3s[layer] = slope.astype(F32)
        normed, scale = layer_norm_parts(dot(value, n_out[layer]) + bias(layer, 4))
        xh2s[layer] = normed
        rs2s[layer] = jnp.broadcast_to(scale, (ROWS, D))
        return (own.astype(F32) + normed * gain(layer, 1)).astype(BF16)

    for layer in range(LAYERS):
        following = forward(layer, (later_uses, later_weights)[layer])
        if layer + 1 < LAYERS:
            state[layer + 1] = following
        else:
            refs["state_v"][...] = following
            put_result("state_v", "state_o")

    def put_term(group, index, values):
        refs["terms_" + group][index * D : index * D + D, :] = values.astype(BF16)

    def reduce_start(group):
        terms, arriving = refs["terms_" + group], refs["rs_in_" + group]
        chunk = arriving.shape[1]
        copies = []
        for step in range(1, ny):
            peer = lax.rem(b + step, ny)
            rows = pl.ds(pl.multiple_of(peer * chunk, chunk), chunk)
            sems = (refs["rs_s_" + group].at[step - 1], refs["rs_r_" + group].at[step - 1])
            copies.append(remote(terms.at[rows], arriving.at[step - 1], *sems, (a, peer)))
        for copy in copies:
            copy.start()
        everything.extend(copies)
        return copies

    def exchange_start(group, reducing):
        terms, arriving, summed = refs["terms_" + group], refs["rs_in_" + group], refs["ar_buf_" + group]
        chunk = arriving.shape[1]
        landed(reducing)
        total = terms[pl.ds(pl.multiple_of(b * chunk, chunk), chunk), :].astype(F32)
        for step in range(ny - 1):
            total = total + arriving[step].astype(F32)
        summed[a] = total.astype(BF16)
        out, come = [], []
        for step in range(1, nx):
            peer = lax.rem(a + step, nx)
            source = lax.rem(a + (nx - step), nx)
            sems = (refs["ar_s_" + group].at[step - 1], refs["ar_r_" + group].at[step - 1])
            out.append(remote(summed.at[a], summed.at[a], *sems, (peer, b)))
            come.append(remote(summed.at[source], summed.at[source], *sems, (peer, b)))
        for copy in out:
            copy.start()
        everything.extend(out)
        return come

    def spread_start(group, exchanging):
        summed, final = refs["ar_buf_" + group], refs["final_" + group]
        landed(exchanging)
        total = summed[0].astype(F32)
        for step in range(1, nx):
            total = total + summed[step].astype(F32)
        final[b] = total.astype(BF16)
        out, come = [], []
        for step in range(1, ny):
            peer = lax.rem(b + step, ny)
            source = lax.rem(b + (ny - step), ny)
            sems = (refs["ag_s_" + group].at[step - 1], refs["ag_r_" + group].at[step - 1])
            out.append(remote(final.at[b], final.at[b], *sems, (a, peer)))
            come.append(remote(final.at[source], final.at[source], *sems, (a, peer)))
        for copy in out:
            copy.start()
        everything.extend(out)
        return come

    vectors = []

    def backward(layer, cotangent, before_edges):
        own = state[layer]
        normed = xh2s[layer]
        lifted = cotangent * gain(layer, 1)
        grad_gain_node = jnp.sum(cotangent * normed, axis=0, keepdims=True)
        inner = jnp.mean(lifted * normed, axis=1, keepdims=True)
        grad = rs2s[layer] * (lifted - jnp.mean(lifted, axis=1, keepdims=True) - normed * inner)
        grad_b4 = jnp.sum(grad, axis=0, keepdims=True)
        grad = grad.astype(BF16)
        put_term("early", NODE_TERMS[layer] + 2, dot_tn(nhs[layer], grad))
        grad = dot_nt(grad, n_out[layer]) * (d3s[layer] * 0.5)
        grad_b3 = jnp.sum(grad, axis=0, keepdims=True)
        grad = grad.astype(BF16)
        put_term("early", NODE_TERMS[layer], dot_tn(own, grad))
        put_term("early", NODE_TERMS[layer] + 1, dot_tn(agg[layer], grad))
        own_grad = cotangent + dot_nt(grad, n_in[layer, 0])
        grad_agg = dot_nt(grad, n_in[layer, 1])
        grad_gain_edge = jnp.sum(grad_agg * agg_raw[layer], axis=0, keepdims=True)
        lifted = grad_agg * gain(layer, 0)
        dxc[...] = lifted - jnp.mean(lifted, axis=1, keepdims=True)
        g_recv[...] = jnp.zeros((ROWS, D), F32)
        dsend[...] = jnp.zeros((PLACES, 2 * D), F32)
        dw_out[...] = jnp.zeros((D, D), F32)
        dw_mid[...] = jnp.zeros((D, D), F32)
        db_out[...] = jnp.zeros((8, 2 * D), F32)
        db_mid[...] = jnp.zeros((8, 2 * D), F32)
        before_edges()

        later = layer == LAYERS - 1
        lowest = HALF if later else 0

        def add_hidden(total, hidden, grad):
            total[...] += dot_tn(hidden[:, :D], grad[:, :D]) + dot_tn(hidden[:, D:], grad[:, D:])

        def chain(j, first):
            rows = slice(first, first + BLOCK)
            lift = twice(dxc[rows])
            unit = xhs[layer, j, rows].astype(F32)
            shared = dot((lift * unit).astype(BF16), ones[...])
            yield
            grad = rss[layer, j, rows].astype(F32) * (lift - unit * shared)
            db_out[...] += partial_sums(grad)
            grad = grad.astype(BF16)
            product = dot(grad, w_out_t[layer])
            if later:
                hits[j, rows, HALF:] = grad
            else:
                add_hidden(dw_out, h2s[layer, j, rows], grad)
            yield
            grad = product * d2s[layer, j, rows].astype(F32)
            db_mid[...] += partial_sums(grad)
            grad = grad.astype(BF16)
            product = dot(grad, w_mid_t[layer])
            if later:
                hits[j + PAIRS, rows, HALF:] = grad
            else:
                add_hidden(dw_mid, h1s[layer, j, rows], grad)
            yield
            grad = product * d1s[layer, j, rows].astype(F32)
            g_recv[rows] += grad[:, :D] + grad[:, D:]
            scattered = None
            for part in range(2):
                k = j + part * PAIRS
                piece = grad[:, part * D : part * D + D]
                high = upper[k, rows] > 0.5
                split = jnp.concatenate([jnp.where(high, 0.0, piece), jnp.where(high, piece, 0.0)], axis=1)
                split = split.astype(BF16)
                if later:
                    hits[k, rows, :HALF] = split
                added = dot(hits_t[k, lowest:, rows], split)
                scattered = added if scattered is None else scattered + added
            dsend[lowest:] += scattered

        staggered(chain, BACKWARD_PAIRS)
        halo_grad = dsend[HALF:].astype(BF16)
        halo_grad = jnp.concatenate([halo_grad[:, :D], halo_grad[:, D:]], axis=0)

        def send_back():
            ret_out[layer] = dot_nt(halo_grad, e_in[layer, 1]).astype(BF16)
            copies = swap_halo(ret_out.at[layer], ret_in.at[layer], ret_s.at[layer], ret_r.at[layer], -1)
            everything.extend(copies)
            return copies

        if later:
            returning = send_back()

            def rest(j, first):
                rows = slice(first, first + BLOCK)
                dsend[:HALF] += sum(dot(hits_t[k, :HALF, rows], hits[k, rows, :HALF]) for k in (j, j + PAIRS))
                add_hidden(dw_out, h2s[layer, j, rows], hits[j, rows, HALF:])
                add_hidden(dw_mid, h1s[layer, j, rows], hits[j + PAIRS, rows, HALF:])
                yield

            staggered(rest, 2)
        send_own = dsend[:HALF].astype(BF16)
        send_own = jnp.concatenate([send_own[:, :D], send_own[:, D:]], axis=0)
        term = dot_tn(own, send_own) + dot_tn(halo_in[layer], halo_grad)
        group = EDGE_GROUPS[layer]
        put_term(group, 1, term)
        grad = g_recv[...]
        grad_b0 = jnp.sum(grad, axis=0, keepdims=True)
        grad = grad.astype(BF16)
        put_term(group, 0, dot_tn(own, grad))
        put_term(group, 2, dw_mid[...])
        put_term(group, 3, dw_out[...])
        total_mid = jnp.sum(db_mid[...], axis=0, keepdims=True)
        total_out = jnp.sum(db_out[...], axis=0, keepdims=True)
        vectors.extend([
            grad_b0,
            total_mid[:, :D] + total_mid[:, D:],
            total_out[:, :D] + total_out[:, D:],
            grad_b3,
            grad_b4,
            grad_gain_edge,
            grad_gain_node,
        ])
        if not later:
            late_start()
            returning = send_back()
        own_grad = own_grad + dot_nt(grad, e_in[layer, 0]) + dot_nt(send_own, e_in[layer, 1])
        if not later:
            prepare_end()
        landed(returning)
        own_grad = own_grad + dot(pick_back[...], ret_in[layer])
        return own_grad.astype(BF16)

    sums = {}

    def early_start():
        sums["early"] = reduce_start("early")

    def late_start():
        terms = refs["terms_late"]
        terms[LATE_VECTORS:, :] = jnp.zeros((LATE_ROWS - LATE_VECTORS, D), BF16)
        stacked = jnp.concatenate(vectors + [jnp.zeros((2, D), F32)], axis=0)
        terms[LATE_VECTORS : LATE_VECTORS + 16, :] = stacked.astype(BF16)
        sums["late"] = reduce_start("late")

    def prepare_end():
        sums["early"] = exchange_start("early", sums["early"])
        back_target = jnp.where(from_row == 4.0, -1.0, from_row * CAP + aslot_row)
        hits[0, :SLOTS, :] = one_hot_rows(back_target, SLOTS)
        hits[1] = one_hot_lanes(column(jnp.where(to_row == 4.0, slot_row, -1.0)), ROWS)
        hits[2, :, :POOL] = one_hot_lanes(column(out_target), POOL)
        sums["late"] = exchange_start("late", sums["late"])

    rounded = backward(1, gout[...].astype(F32), lambda: None)
    rounded = backward(0, rounded.astype(F32), early_start)

    back_out[...] = dot(hits[0, :SLOTS, :], rounded).astype(BF16)
    going_back = swap_slots(back_out, back_in, back_s, back_r, -1)
    everything += going_back
    staying = dot(hits[1], rounded)
    sums["early"] = spread_start("early", sums["early"])
    sums["late"] = spread_start("late", sums["late"])
    landed(going_back)
    refs["glat_v"][...] = (staying + dot(hits[2, :, :POOL], back_in[...])).astype(BF16)
    put_result("glat_v", "glat_o")
    landed(sums["early"])
    put_result("final_early", "early_o")
    landed(sums["late"])
    put_result("final_late", "late_o")
    for copy in stored:
        copy.wait()
    for copy in everything:
        copy.wait_send()


def unpack(state, grad_latent, early, late, state_o, glat_o, gein_o, gehid_o, gnin_o, gnout_o, gbia_o, ggai_o):
    state_o[...] = state[...]
    glat_o[...] = grad_latent[...]
    sums = dict(early=early, late=late)

    def matrix(group, index):
        return sums[group][index * D : index * D + D, :].astype(F32)

    for layer in range(LAYERS):
        group, node = EDGE_GROUPS[layer], NODE_TERMS[layer]
        for index in range(2):
            gein_o[layer, index] = matrix(group, index)
            gehid_o[layer, index] = matrix(group, index + 2)
            gnin_o[layer, index] = matrix("early", node + index)
        gnout_o[layer] = matrix("early", node + 2)
    vectors = late[LATE_VECTORS : LATE_VECTORS + 16, :].astype(F32)
    for layer in range(LAYERS):
        first = 7 * (LAYERS - 1 - layer)
        gbia_o[:, layer] = vectors[first : first + 5]
        ggai_o[layer] = vectors[first + 5 : first + 7]


def shards(
    latent, move_to, move_slot, arrive_from, arrive_slot, neighbours, valid_count, face_send, corner_send,
    edge_in, edge_hid, node_in, node_out, biases, gains, grad_out,
):
    nx, ny = lax.axis_size("bx"), lax.axis_size("by")
    vmem = pl.BlockSpec(memory_space=pltpu.VMEM)
    shape = jax.ShapeDtypeStruct
    saved = pltpu.VMEM((LAYERS, PAIRS, ROWS, 2 * D), BF16)
    node = pltpu.VMEM((LAYERS, ROWS, D), F32)
    node_bf = pltpu.VMEM((LAYERS, ROWS, D), BF16)
    wide = pltpu.VMEM((LAYERS, 2 * D, 2 * D), BF16)
    dma = pltpu.SemaphoreType.DMA
    scratch = dict(
        outgoing=pltpu.VMEM((SLOTS, D), BF16),
        arrived=pltpu.VMEM((POOL, D), BF16),
        halo_out=pltpu.VMEM((LAYERS, HALO, D), BF16),
        halo_in=pltpu.VMEM((LAYERS, HALO, D), BF16),
        ret_out=pltpu.VMEM((LAYERS, HALO, D), BF16),
        ret_in=pltpu.VMEM((LAYERS, HALO, D), BF16),
        back_out=pltpu.VMEM((SLOTS, D), BF16),
        back_in=pltpu.VMEM((POOL, D), BF16),
        pick_send=pltpu.VMEM((HALO, ROWS), BF16),
        pick_back=pltpu.VMEM((ROWS, HALO), BF16),
        hits=pltpu.VMEM((K, ROWS, ROWS), BF16),
        hits_t=pltpu.VMEM((K, PLACES, ROWS), BF16),
        upper=pltpu.VMEM((K, ROWS, D), F32),
        count_col=pltpu.VMEM((ROWS, D), F32),
        state=node_bf,
        recv_term=pltpu.VMEM((ROWS, D), F32),
        own_tab=pltpu.VMEM((HALF, 2 * D), BF16),
        halo_tab=pltpu.VMEM((HALF, 2 * D), BF16),
        before=pltpu.VMEM((K, ROWS, D), F32),
        w_mid=wide,
        w_out=wide,
        w_mid_t=wide,
        w_out_t=wide,
        ones=pltpu.VMEM((2 * D, 2 * D), BF16),
        h1s=saved,
        h2s=saved,
        d1s=saved,
        d2s=saved,
        xhs=saved,
        rss=saved,
        acc=pltpu.VMEM((ROWS, D), F32),
        agg=node_bf,
        nhs=node_bf,
        d3s=node,
        xh2s=node,
        rs2s=node,
        dxc=pltpu.VMEM((ROWS, D), F32),
        g_recv=pltpu.VMEM((ROWS, D), F32),
        agg_raw=node,
        dsend=pltpu.VMEM((PLACES, 2 * D), F32),
        dw_out=pltpu.VMEM((D, D), F32),
        dw_mid=pltpu.VMEM((D, D), F32),
        db_out=pltpu.VMEM((8, 2 * D), F32),
        db_mid=pltpu.VMEM((8, 2 * D), F32),
        mig_s=dma((CODES,)),
        mig_r=dma((CODES,)),
        halo_s=dma((LAYERS, 8)),
        halo_r=dma((LAYERS, 8)),
        ret_s=dma((LAYERS, 8)),
        ret_r=dma((LAYERS, 8)),
        back_s=dma((CODES,)),
        back_r=dma((CODES,)),
        load_s=dma((16,)),
        store_s=dma((4,)),
        state_v=pltpu.VMEM((ROWS, D), BF16),
        glat_v=pltpu.VMEM((ROWS, D), BF16),
    )
    for group, total in (("early", EARLY_ROWS), ("late", LATE_ROWS)):
        chunk = total // ny
        scratch["terms_" + group] = pltpu.VMEM((total, D), BF16)
        scratch["rs_in_" + group] = pltpu.VMEM((ny - 1, chunk, D), BF16)
        scratch["ar_buf_" + group] = pltpu.VMEM((nx, chunk, D), BF16)
        scratch["final_" + group] = pltpu.VMEM((ny, chunk, D), BF16)
        for stage, partners in (("rs", ny), ("ar", nx), ("ag", ny)):
            scratch[f"{stage}_s_{group}"] = dma((partners - 1,))
            scratch[f"{stage}_r_{group}"] = dma((partners - 1,))

    def row(values):
        return values.reshape(1, ROWS)

    arguments = (
        latent, row(move_to), row(move_slot), row(arrive_from), row(arrive_slot),
        neighbours.T, row(valid_count), face_send.reshape(4, -1), corner_send.reshape(4, -1),
        edge_in, edge_hid, node_in, node_out, biases.transpose(1, 0, 2), gains, grad_out,
    )
    for name, value in zip(ARGUMENTS, arguments):
        scratch[name] = pltpu.VMEM(value.shape, value.dtype)
    names = ["arg_" + name for name in ARGUMENTS] + list(RESULTS) + list(scratch)
    state, grad_latent, early, late = pl.pallas_call(
        functools.partial(kernel, nx, ny, names),
        out_shape=(
            shape((ROWS, D), BF16),
            shape((ROWS, D), BF16),
            shape((ny, EARLY_ROWS // ny, D), BF16),
            shape((ny, LATE_ROWS // ny, D), BF16),
        ),
        in_specs=[pl.BlockSpec(memory_space=pl.ANY)] * len(ARGUMENTS),
        out_specs=(pl.BlockSpec(memory_space=pl.ANY),) * len(RESULTS),
        scratch_shapes=list(scratch.values()),
        compiler_params=pltpu.CompilerParams(
            collective_id=0, has_side_effects=True, vmem_limit_bytes=62 * 1024 * 1024
        ),
        name="evolve",
    )(*arguments)
    outputs = pl.pallas_call(
        unpack,
        out_shape=(
            shape((ROWS, D), BF16),
            shape((ROWS, D), BF16),
            shape((LAYERS, 2, D, D), F32),
            shape((LAYERS, 2, D, D), F32),
            shape((LAYERS, 2, D, D), F32),
            shape((LAYERS, D, D), F32),
            shape((5, LAYERS, D), F32),
            shape((LAYERS, 2, D), F32),
        ),
        in_specs=[vmem] * 4,
        out_specs=(vmem,) * 8,
        name="unpack",
    )(state, grad_latent, early.reshape(EARLY_ROWS, D), late.reshape(LATE_ROWS, D))
    return *outputs[:6], outputs[6].transpose(1, 0, 2), outputs[7]


def solution(mesh):
    both = ("bx", "by")
    rows, wide, grid = P(both), P(both, None), P("bx", "by", None, None)
    return jax.shard_map(
        shards,
        mesh=mesh,
        in_specs=(wide, rows, rows, rows, rows, wide, rows, grid, grid, P(), P(), P(), P(), P(), P(), wide),
        out_specs=(wide, wide, P(), P(), P(), P(), P(), P()),
        check_vma=False,
    )
```
